32 devices in a mesh: snap: 4 (over y, core), slab: 8 (over z, x).
Axes of the slice: x: 2, y: 2, z: 4, core: 2. Of those that a mesh axis runs over, the one named last changes fastest.
Arguments:
- velocity: bfloat16 [64, 3, 64, 16, 512], P('snap', None, 'slab'), may hold values from -6 to 6
- phase_bins: int32 [64], P('snap'), may hold values from 0 to 179, as said below
Outputs:
- coefficients: float32 [3, 3, 4, 64, 16, 512], P(None, None, None, 'slab', None, 'snap')
The draws below stay inside these ranges and needn't reach their ends.
Inputs may be any that keep to these rules, and one draw needn't show every extreme that they name: `phase_bins`: no two snapshots share a bin, and the bins of all snapshots spread over the whole revolution.
All inputs are finite; a program needn't handle non-finite values.
Results may differ from the reference program's by a relative error of at most 0.0003.
Values may be sent and summed in bfloat16 or wider, within the bound.
No kernel may reach another device: no remote copies, remote signals or barrier semaphores. Data moves between devices by JAX's collectives and lax.ppermute only.
A program may use at most 128 MiB of HBM per device.

```python
import jax
import jax.numpy as jnp
from jax import lax

NY = 16
NZ = 512
BINS = 180
BASIS = 3
ORDERS = 4
NSNAP = 64
NX = 64


def draw_phase_bins(key, part):
    first_key = jax.random.fold_in(key, 11)
    second_key = jax.random.fold_in(key, 23)
    strata = jax.random.permutation(first_key, jnp.arange(NSNAP, dtype=jnp.int32))
    jitter = jax.random.randint(second_key, (NSNAP,), 0, max(BINS // NSNAP, 1), dtype=jnp.int32)
    return (strata * BINS // NSNAP + jitter).astype(jnp.int32)


def block_levels(rng, dims, pieces, smallest, top_value):
    factor_of = 1.0
    for dim, shards_of in pieces:
        steps = jax.random.uniform(jax.random.fold_in(jax.random.fold_in(rng, 6), dim), (shards_of,), jnp.float32, smallest / len(pieces), top_value / len(pieces))
        factor_of = factor_of * jnp.repeat(jnp.exp(steps), dims[dim] // shards_of).reshape((-1,) + (1,) * (len(dims) - 1 - dim))
    return factor_of


def normal_values(key, shape, width, bound, split=(), kind=jnp.bfloat16):
    loudness = block_levels(key, shape, split, -0.22, 0.18) if split else 1.0
    drawn = jax.random.normal(key, shape, jnp.float32) * width * loudness
    return jnp.minimum(jnp.maximum(drawn, -bound), bound).astype(kind)


def setup_inputs(seed: int = 0) -> dict:
    streams_of = jax.random.split(jax.random.key(seed), 3)
    velocity = normal_values(streams_of[0], (NSNAP, 3, NX, NY, NZ), 1.0, 6.0, ((0, 4), (2, 8)))
    phase_bins = draw_phase_bins(jax.random.fold_in(streams_of[2], 71), 0)
    return {"velocity": velocity, "phase_bins": phase_bins}


inv_spacing = 0.75


def central(padded, direction):
    extent = padded.shape[-3:]
    leading = [slice(None)] * (padded.ndim - 3)

    def shifted(offset):
        window = [slice(2, extent[0] - 2), slice(2, extent[1] - 2), slice(2, extent[2] - 2)]
        window[direction] = slice(offset, extent[direction] - 4 + offset)
        return padded[tuple(leading + window)].astype(jnp.float32)

    return (8.0 * (shifted(3) - shifted(1)) - (shifted(4) - shifted(0))) * (inv_spacing / 12.0)


def vorticity_of(comp_u, comp_v, comp_w):
    omega_x = central(comp_w, 1) - central(comp_v, 2)
    omega_y = central(comp_u, 2) - central(comp_w, 0)
    omega_z = central(comp_v, 0) - central(comp_u, 1)
    return jnp.stack([omega_x, omega_y, omega_z], axis=-4)


def basis_weights(phase_bins):
    centers = (jnp.arange(BINS, dtype=jnp.float32) + 0.5) * (2.0 * jnp.pi / BINS)
    table = jnp.stack([jnp.ones_like(centers), jnp.cos(centers), jnp.sin(centers)], axis=1)
    onehot = (phase_bins[:, None] == jnp.arange(BINS, dtype=jnp.int32)[None, :]).astype(jnp.float32)
    return jnp.dot(onehot, table, precision=lax.Precision.HIGHEST)


def invert_three(gram):
    g00, g01, g02 = gram[0, 0], gram[0, 1], gram[0, 2]
    g10, g11, g12 = gram[1, 0], gram[1, 1], gram[1, 2]
    g20, g21, g22 = gram[2, 0], gram[2, 1], gram[2, 2]
    c00 = g11 * g22 - g12 * g21
    c01 = g02 * g21 - g01 * g22
    c02 = g01 * g12 - g02 * g11
    c10 = g12 * g20 - g10 * g22
    c11 = g00 * g22 - g02 * g20
    c12 = g02 * g10 - g00 * g12
    c20 = g10 * g21 - g11 * g20
    c21 = g01 * g20 - g00 * g21
    c22 = g00 * g11 - g01 * g10
    determinant = g00 * c00 + g01 * c10 + g02 * c20
    adjugate = jnp.stack([jnp.stack([c00, c01, c02]), jnp.stack([c10, c11, c12]), jnp.stack([c20, c21, c22])])
    return adjugate / determinant


def reference(velocity, phase_bins):
    weights = basis_weights(phase_bins)

    def accumulate(total, inputs):
        snapshot_field, weight_row = inputs
        padded = jnp.pad(snapshot_field.astype(jnp.float32), ((0, 0), (2, 2), (2, 2), (2, 2)))
        omega = vorticity_of(padded[0], padded[1], padded[2])
        squared = omega * omega
        powers = jnp.stack([omega, squared, squared * omega, squared * squared], axis=1)
        return total + weight_row[:, None, None, None, None, None] * powers[None], None

    start = jnp.zeros((BASIS, 3, ORDERS, NX, NY, NZ), jnp.float32)
    sums, _ = lax.scan(accumulate, start, (velocity, weights))
    gram = jnp.dot(weights.T, weights, precision=lax.Precision.HIGHEST)
    inverse = invert_three(gram)
    return jnp.einsum('ij,j...->i...', inverse, sums, precision=lax.Precision.HIGHEST)
```

```python
import functools

import jax
import jax.numpy as jnp
import numpy as np
from jax import lax
from jax.experimental import pallas as pl
from jax.experimental.pallas import tpu as pltpu
from jax.sharding import PartitionSpec as P

BINS = 180
ORDERS = 4
TAPS = ((-2, 1.0), (-1, -8.0), (1, 8.0), (2, -1.0))
STEP = 0.75 / 12.0
VMEM = 48 * 2**20


def band(size):
    matrix = np.zeros((size, size), np.float32)
    for offset, factor in TAPS:
        matrix += factor * np.eye(size, k=offset, dtype=np.float32)
    return matrix


def phase_table():
    centers = (jnp.arange(BINS, dtype=jnp.float32) + 0.5) * (2.0 * jnp.pi / BINS)
    return jnp.stack([jnp.ones_like(centers), jnp.cos(centers), jnp.sin(centers)], axis=1)


def basis_weights(phase_bins):
    onehot = (phase_bins[:, None] == jnp.arange(BINS, dtype=jnp.int32)[None, :]).astype(jnp.float32)
    return jnp.dot(onehot, phase_table(), precision=lax.Precision.HIGHEST)


def invert_three(gram):
    g00, g01, g02 = (gram[0, 0], gram[0, 1], gram[0, 2])
    g10, g11, g12 = (gram[1, 0], gram[1, 1], gram[1, 2])
    g20, g21, g22 = (gram[2, 0], gram[2, 1], gram[2, 2])
    c00 = g11 * g22 - g12 * g21
    c01 = g02 * g21 - g01 * g22
    c02 = g01 * g12 - g02 * g11
    c10 = g12 * g20 - g10 * g22
    c11 = g00 * g22 - g02 * g20
    c12 = g02 * g10 - g00 * g12
    c20 = g10 * g21 - g11 * g20
    c21 = g01 * g20 - g00 * g21
    c22 = g00 * g11 - g01 * g10
    determinant = g00 * c00 + g01 * c10 + g02 * c20
    adjugate = jnp.stack(
        [jnp.stack([c00, c01, c02]), jnp.stack([c10, c11, c12]), jnp.stack([c20, c21, c22])]
    )
    return adjugate / determinant


def spread_weights(bins, table, weight):
    for s in range(weight.shape[0]):
        row = bins[s] * 2
        weight[s, 0] = jnp.full((8, 128), table[row], jnp.float32)
        weight[s, 1] = jnp.full((8, 128), table[row + 1], jnp.float32)


def sum_powers(field, weight, lane, out, cell):
    snaps = weight.shape[0]
    rows = field.shape[0] // snaps
    for half in range(rows // 8):
        total = [None] * (3 * ORDERS)
        for s in range(snaps):
            first = field[pl.ds(s * rows + half * 8, 8), pl.ds(lane, 128)]
            second = first * first
            powers = (first, second, second * first, second * second)
            for j in range(3):
                for k in range(ORDERS):
                    term = powers[k] if j == 0 else powers[k] * weight[s, j - 1]
                    at = j * ORDERS + k
                    total[at] = term if s == 0 else total[at] + term
        for j in range(3):
            for k in range(ORDERS):
                out[cell, j, k, pl.ds(half * 8, 8), :] = total[j * ORDERS + k] * STEP ** (k + 1)


def sum_blocks(field, weight, place, outs, cell):
    for block, out in enumerate(outs):
        sum_powers(field, weight, pl.multiple_of(place[block] * 128, 128), out, cell)


def flat(block):
    return block.reshape(block.shape[0] * block.shape[1], block.shape[2])


def streamwise_kernel(bins, table, place, along_y, along_z, v, w, *refs):
    outs, (weight, field) = refs[:4], refs[4:]

    @pl.when(pl.program_id(0) == 0)
    def _():
        spread_weights(bins, table, weight)

    field[...] = jnp.dot(along_y[...], flat(w[:, 0, 0]), preferred_element_type=jnp.float32) - jnp.dot(
        flat(v[:, 0, 0]), along_z[...], preferred_element_type=jnp.float32
    )
    sum_blocks(field, weight, place, outs, 0)


def difference_x(planes, q, s):
    taps = [planes(s, q + offset).astype(jnp.float32) for offset in (0, 1, 3, 4)]
    return 8.0 * (taps[2] - taps[1]) - (taps[3] - taps[0])


def cross_fields(along_y, along_z, u, planes_v, planes_w, q, field_y, field_z, snaps, rows):
    field_y[...] = jnp.dot(u, along_z[...], preferred_element_type=jnp.float32)
    field_z[...] = jnp.dot(along_y[...], u, preferred_element_type=jnp.float32)
    for s in range(snaps):
        at = pl.ds(s * rows, rows)
        field_y[at, :] = field_y[at, :] - difference_x(planes_w, q, s)
        field_z[at, :] = difference_x(planes_v, q, s) - field_z[at, :]


def inner_kernel(bins, table, place, along_y, along_z, *refs):
    u, vs, ws, outs = refs[0], refs[1:5], refs[5:9], refs[9:13]
    weight, field_y, field_z = refs[13:]

    @pl.when(pl.program_id(0) == 0)
    def _():
        spread_weights(bins, table, weight)

    slot = {0: 0, 1: 1, 3: 2, 4: 3}
    cross_fields(
        along_y, along_z, flat(u[:, 0, 0]),
        lambda s, at: vs[slot[at]][s, 0, 0],
        lambda s, at: ws[slot[at]][s, 0, 0],
        0, field_y, field_z, u.shape[0], u.shape[3],
    )
    sum_blocks(field_y, weight, place, outs, 0)
    sum_blocks(field_z, weight, place, outs, 1)


def edge_kernel(bins, table, place, side, along_y, along_z, velocity, halo, *refs):
    outs = refs[:4]
    weight, field_y, field_z, center, cross, sems = refs[4:]
    q = pl.program_id(0)
    base, own, beyond = side[0], side[1], side[2]

    @pl.when(q == 0)
    def _():
        copies = [
            pltpu.make_async_copy(
                velocity.at[:, pl.ds(0, 1), pl.ds(base, 2)], center, sems.at[0]
            ),
            pltpu.make_async_copy(
                velocity.at[:, pl.ds(1, 2), pl.ds(own, 4)], cross.at[:, :, pl.ds(2 - beyond, 4)], sems.at[1]
            ),
            pltpu.make_async_copy(halo, cross.at[:, :, pl.ds(beyond * 2, 2)], sems.at[2]),
        ]
        for copy in copies:
            copy.start()
        spread_weights(bins, table, weight)
        for copy in copies:
            copy.wait()

    cross_fields(
        along_y, along_z, flat(center[:, 0, q]),
        lambda s, at: cross[s, 0, at],
        lambda s, at: cross[s, 1, at],
        q, field_y, field_z, center.shape[0], center.shape[3],
    )
    sum_blocks(field_y, weight, place, outs, 0)
    sum_blocks(field_z, weight, place, outs, 1)


def finish_kernel(cells, of, inverse, *refs):
    keep, core, across, out = refs[0], refs[1], refs[2], refs[-1]
    for k in range(ORDERS):
        sums = [keep[0, j, k] + core[0, j, k] + across[0, j, k] for j in range(3)]
        for i in range(3):
            out[i, 0, k, 0] = inverse[3 * i] * sums[0] + inverse[3 * i + 1] * sums[1] + inverse[3 * i + 2] * sums[2]


def smem():
    return pl.BlockSpec(memory_space=pltpu.SMEM)


def local(velocity, phase_bins):
    snaps, _, planes, rows, lanes = velocity.shape
    snap, slab = lax.axis_index("snap"), lax.axis_index("slab")
    n_snap, n_slab = lax.axis_size("snap"), lax.axis_size("slab")
    width = lanes // n_snap
    odd = lax.rem(slab, 2)

    pairs = [(i, i ^ 1) for i in range(n_slab)]
    others = [(i, i + 1) for i in range(1, n_slab - 1, 2)]
    others = others + [(j, i) for i, j in others]
    far = planes - 2

    def edge_planes(start):
        return lax.dynamic_slice(velocity, (0, 1, start, 0, 0), (snaps, 2, 2, rows, lanes))

    halo_near = lax.ppermute(edge_planes(jnp.where(odd == 0, far, 0)), "slab", pairs)
    halo_far = lax.ppermute(edge_planes(jnp.where(odd == 0, 0, far)), "slab", others)

    chip, core = lax.div(snap, 2), lax.rem(snap, 2)
    there, here = (1 - chip) * 2, chip * 2
    place = jnp.stack([there + core, here + core, there + 1 - core, here + 1 - core]).astype(jnp.int32)
    core_pairs = [(i, i ^ 1) for i in range(n_snap)]
    chip_pairs = [(i, (i + 2) % n_snap) for i in range(n_snap)]

    table = phase_table()[:, 1:].reshape(-1)
    along_y = jnp.asarray(np.kron(np.eye(snaps, dtype=np.float32), band(rows)), jnp.bfloat16)
    along_z = jnp.asarray(band(lanes).T, jnp.bfloat16)
    weight = pltpu.VMEM((snaps, 2, 8, 128), jnp.float32)
    field = pltpu.VMEM((snaps * rows, lanes), jnp.float32)
    constants = [
        pl.BlockSpec((snaps * rows, snaps * rows), lambda p: (0, 0)),
        pl.BlockSpec((lanes, lanes), lambda p: (0, 0)),
    ]

    def plane(component, offset):
        return pl.BlockSpec((snaps, 1, 1, rows, lanes), lambda p: (0, component, p + offset, 0, 0))

    def sums(steps, cells):
        shape = jax.ShapeDtypeStruct((steps * cells, 3, ORDERS, rows, width), jnp.float32)
        spec = pl.BlockSpec((cells, 3, ORDERS, rows, width), lambda p: (p, 0, 0, 0, 0))
        return {"out_shape": [shape] * 4, "out_specs": [spec] * 4, "grid": (steps,)}

    def params(cells):
        flops = cells * snaps * rows * lanes * 30
        return {
            "compiler_params": pltpu.CompilerParams(vmem_limit_bytes=VMEM),
            "cost_estimate": pl.CostEstimate(flops=flops, bytes_accessed=cells * 12 * rows * lanes * 4, transcendentals=0),
        }

    with jax.named_scope("streamwise"):
        first = pl.pallas_call(
            streamwise_kernel,
            in_specs=[smem(), smem(), smem(), *constants, plane(1, 0), plane(2, 0)],
            scratch_shapes=[weight, field],
            **sums(planes, 1), **params(planes),
        )(phase_bins, table, place, along_y, along_z, velocity, velocity)

    with jax.named_scope("inner"):
        inner = pl.pallas_call(
            inner_kernel,
            in_specs=[smem(), smem(), smem(), *constants, plane(0, 2)]
            + [plane(c, offset) for c in (1, 2) for offset in (0, 1, 3, 4)],
            scratch_shapes=[weight, field, field],
            **sums(planes - 4, 2), **params(2 * planes - 8),
        )(phase_bins, table, place, along_y, along_z, *[velocity] * 9)

    def edge(halo, high):
        side = jnp.stack([high * far, high * (planes - 4), high * 2]).astype(jnp.int32)
        return pl.pallas_call(
            edge_kernel,
            in_specs=[smem(), smem(), smem(), smem(), *constants]
            + [pl.BlockSpec(memory_space=pl.ANY)] * 2,
            scratch_shapes=[
                weight, field, field,
                pltpu.VMEM((snaps, 1, 2, rows, lanes), velocity.dtype),
                pltpu.VMEM((snaps, 2, 6, rows, lanes), velocity.dtype),
                pltpu.SemaphoreType.DMA((3,)),
            ],
            **sums(2, 2), **params(4),
        )(phase_bins, table, place, side, along_y, along_z, velocity, halo)

    with jax.named_scope("edge_near"):
        near = edge(halo_near, 1 - odd)
    with jax.named_scope("edge_far"):
        outer = edge(halo_far, odd)

    all_weights = basis_weights(lax.all_gather(phase_bins, "snap", axis=0, tiled=True))
    gram = jnp.dot(all_weights.T, all_weights, precision=lax.Precision.HIGHEST)
    inverse = invert_three(gram).reshape(-1)

    def exchange(parts):
        keep_there, keep_here, send_there, send_here = parts
        core_there = lax.ppermute(send_there, "snap", core_pairs)
        core_here = lax.ppermute(send_here, "snap", core_pairs)
        across = lax.ppermute(keep_there + core_there, "snap", chip_pairs)
        return keep_here, core_here, across

    out_shape = jax.ShapeDtypeStruct((3, 3, ORDERS, planes, rows, width), jnp.float32)

    def finish(parts, out, base, where):
        cells = parts[0].shape[0]
        cell = pl.BlockSpec((1, 3, ORDERS, rows, width), lambda p, base: (p, 0, 0, 0, 0))

        def target(p, base):
            component, at = where(p, base)
            return 0, component, 0, at, 0, 0

        def body(base, inverse, *refs):
            finish_kernel(cells, where, inverse, *refs)

        ops = [inverse, *parts] + ([] if out is None else [out])
        return pl.pallas_call(
            body,
            out_shape=out_shape,
            grid_spec=pltpu.PrefetchScalarGridSpec(
                num_scalar_prefetch=1,
                grid=(cells,),
                in_specs=[smem()] + [cell] * 3 + ([] if out is None else [pl.BlockSpec(memory_space=pl.ANY)]),
                out_specs=pl.BlockSpec((3, 1, ORDERS, 1, rows, width), target),
            ),
            input_output_aliases={} if out is None else {5: 0},
            compiler_params=pltpu.CompilerParams(vmem_limit_bytes=VMEM),
        )(base, *ops)

    def pair_of(p, base):
        return 1 + lax.rem(p, 2), base[0] + lax.div(p, 2)

    def base_of(value):
        return jnp.asarray(value, jnp.int32).reshape(1)

    out = finish(exchange(first), None, base_of(0), lambda p, base: (0, p))
    out = finish(exchange(inner), out, base_of(2), pair_of)
    out = finish(exchange(near), out, base_of((1 - odd) * far), pair_of)
    return finish(exchange(outer), out, base_of(odd * far), pair_of)


def solution(mesh):
    in_specs = (P("snap", None, "slab", None, None), P("snap"))
    out_specs = P(None, None, None, "slab", None, "snap")
    return jax.shard_map(local, mesh=mesh, in_specs=in_specs, out_specs=out_specs, check_vma=False)
```

```python
import jax
import jax.numpy as jnp
import numpy as np
from jax import lax
from jax.experimental import pallas as pl
from jax.experimental.pallas import tpu as pltpu
from jax.sharding import PartitionSpec as P

BINS = 180
ORDERS = 4
TAPS = ((-2, 1.0), (-1, -8.0), (1, 8.0), (2, -1.0))
STEP = 0.75 / 12.0
PARAMS = {
    "compiler_params": pltpu.CompilerParams(vmem_limit_bytes=60 * 2**20),
    "cost_estimate": pl.CostEstimate(flops=1, bytes_accessed=1, transcendentals=0),
}
LEVELS = 32766.0
TINY = 1e-30
BLOCKS, NEAR, FAR = 0, 3, 8
EDGE, OWN, OWN_AT, HALO_AT, EDGE_AT = range(5)


def band(size):
    matrix = np.zeros((size, size), np.float32)
    for offset, factor in TAPS:
        matrix += factor * np.eye(size, k=offset, dtype=np.float32)
    return matrix


def five_planes(width):
    matrix = np.zeros((5, width, width), np.float32)
    for offset, factor in TAPS:
        matrix[2 + offset] = factor * np.eye(width, dtype=np.float32)
    return matrix.reshape(5 * width, width)


def phase_table():
    centers = (np.arange(BINS, dtype=np.float32) + np.float32(0.5)) * np.float32(2.0 * np.pi / BINS)
    return np.stack([np.cos(centers), np.sin(centers)], axis=1).astype(np.float32)


def invert_kernel(bins, table, inverse):
    g00 = jnp.float32(bins.shape[0])
    g01 = g02 = g11 = g12 = g22 = jnp.float32(0.0)
    for s in range(bins.shape[0]):
        cosine, sine = table[bins[s] * 2], table[bins[s] * 2 + 1]
        g01, g02 = g01 + cosine, g02 + sine
        g11, g12, g22 = g11 + cosine * cosine, g12 + cosine * sine, g22 + sine * sine
    g00, g01, g02, g11, g12, g22 = (jnp.full(inverse.shape[1:], g, jnp.float32) for g in (g00, g01, g02, g11, g12, g22))
    c00 = g11 * g22 - g12 * g12
    c01 = g02 * g12 - g01 * g22
    c02 = g01 * g12 - g02 * g11
    c11 = g00 * g22 - g02 * g02
    c12 = g02 * g01 - g00 * g12
    c22 = g00 * g11 - g01 * g01
    determinant = g00 * c00 + g01 * c01 + g02 * c02
    for i, entry in enumerate((c00, c01, c02, c01, c11, c12, c02, c12, c22)):
        inverse[i] = entry / determinant


def spread_weights(bins, table, weight):
    for s in range(weight.shape[0]):
        row = bins[s] * 2
        weight[s, 0] = jnp.full((8, 128), table[row], jnp.float32)
        weight[s, 1] = jnp.full((8, 128), table[row + 1], jnp.float32)


def power_sums(field, weight, lane, rows, store):
    for half in range(rows // 8):
        total = [None] * (3 * ORDERS)
        for s in range(weight.shape[0]):
            first = field[pl.ds(s * rows + half * 8, 8), pl.ds(lane, 128)]
            second = first * first
            powers = (first, second, second * first, second * second)
            for j in range(3):
                for k in range(ORDERS):
                    term = powers[k] if j == 0 else powers[k] * weight[s, j - 1]
                    at = j * ORDERS + k
                    total[at] = term if s == 0 else total[at] + term
        scaled = [[total[j * ORDERS + k] * STEP ** (k + 1) for k in range(ORDERS)] for j in range(3)]
        store(pl.ds(half * 8, 8), scaled)


def pair_sums(field, weight, rows, there, here, cell):
    for lane, target in ((0, there), (128, here)):
        def store(at, sums, target=target):
            for j in range(3):
                for k in range(ORDERS):
                    target[k, j, cell, at, :] = sums[j][k]

        power_sums(field, weight, lane, rows, store)


def encode(sums, exponents, code, groups):
    cells, rows = sums.shape[2:4]
    exponents[...] = jnp.zeros(exponents.shape, jnp.float32)
    for n in range(ORDERS * 3):
        for g, (start, stop) in enumerate(groups):
            value = sums[n // 3, n % 3, start:stop]
            top = jnp.max(jnp.max(jnp.abs(value), axis=0), axis=0, keepdims=True)
            exponent = jnp.ceil(jnp.log(jnp.maximum(top, TINY)) * np.float32(1.0 / np.log(2.0)))
            rounded = jnp.round(value * (jnp.exp2(-exponent) * LEVELS))
            code[n * cells + start : n * cells + stop] = rounded.astype(jnp.int32).astype(jnp.int16)
            exponents[pl.ds(n * len(groups) + g, 1), :] = exponent
    last = exponents[...].reshape(exponents.shape[0] // rows, rows, exponents.shape[1])
    code[ORDERS * 3 * cells :] = last.astype(jnp.int32).astype(jnp.int16)


def decode_scales(code, scales):
    exponents = code.astype(jnp.int32).astype(jnp.float32)
    scales[...] = (jnp.exp2(exponents) * (1.0 / LEVELS)).reshape(scales.shape)


def flat(block):
    return block.reshape(block.shape[0] * block.shape[1], block.shape[2])


def product(a, b):
    return jnp.dot(a, b, preferred_element_type=jnp.float32)


def lanes_from(start, size):
    return pl.ds(pl.multiple_of(start, 128), size)


def block_of(where, b):
    return lanes_from(where[BLOCKS + b] * 128, 128)


def make_copies(pairs, sems):
    return [pltpu.make_async_copy(source, target, sems.at[i]) for i, (source, target) in enumerate(pairs)]


def run_copies(pairs, sems, meanwhile=lambda: None):
    copies = make_copies(pairs, sems)
    for copy in copies:
        copy.start()
    meanwhile()
    for copy in copies:
        copy.wait()


def both_along_y(along_y, block):
    return jnp.concatenate([product(along_y[...], flat(block[g])) for g in range(block.shape[0])], axis=0)


def rows_of(block):
    return block.reshape(-1, block.shape[-1])


def fill_x(field, along_y, along_z, v, w):
    field[...] = both_along_y(along_y, w) - product(rows_of(v), along_z[...])


def fill_y(field, along_x, along_z, u, w_planes):
    field[...] = product(rows_of(u), along_z[...]) - product(rows_of(w_planes), along_x[...])


def fill_z(field, along_x, along_y, u, v_planes):
    field[...] = product(rows_of(v_planes), along_x[...]) - both_along_y(along_y, u)


def inside_kernel(bins, table, where, along_x, along_y, along_z, own, other, code, here, there, exponents, weight, *refs):
    fields, (u_full, v_full, v_half, w_half, sems) = refs[:4], refs[4:]
    step = pl.program_id(0)
    planes, rows, pair = v_full.shape[1], v_full.shape[3], fields[0].shape[1]
    steps = planes // 2

    def of_plane(p):
        pairs = []
        for g, source in enumerate((own, other)):
            pairs.append((source.at[:, 1, p], v_full.at[g, p]))
            for b in range(2):
                lane = pl.ds(p * pair + b * 128, 128)
                pairs.append((source.at[:, 1, p, :, block_of(where, b)], v_half.at[g, :, :, lane]))
                pairs.append((source.at[:, 2, p, :, block_of(where, b)], w_half.at[g, :, :, lane]))
            if 2 <= p < planes - 2:
                pairs.append((source.at[:, 0, p], u_full.at[g, p - 2]))
        return make_copies(pairs, sems.at[p])

    def streamwise(field, p):
        fill_x(field, along_y, along_z, v_full[:, p], w_half[:, :, :, lanes_from(p * pair, pair)])

    @pl.when(step == 0)
    def _():
        for p in range(planes):
            for copy in of_plane(p):
                copy.start()
        spread_weights(bins, table, weight)
        for copy in of_plane(0):
            copy.wait()
        streamwise(fields[0], 0)

    for q in range(steps):
        @pl.when(step == q)
        def _(q=q):
            for p in range(1, planes - steps + 1) if q == 0 else (planes - steps + q,):
                for copy in of_plane(p):
                    copy.wait()

    five = lanes_from(step * pair, 5 * pair)
    streamwise(fields[1], 2 * step + 1)
    pair_sums(fields[0], weight, rows, there, here, 2 * step)
    fill_y(fields[2], along_x, along_z, u_full[:, step], w_half[:, :, :, five])
    pair_sums(fields[1], weight, rows, there, here, 2 * step + 1)
    halves = jnp.concatenate([u_full[:, step, :, :, block_of(where, b)] for b in range(2)], axis=-1)
    fill_z(fields[3], along_x, along_y, halves, v_half[:, :, :, five])
    pair_sums(fields[2], weight, rows, there, here, planes + step)
    streamwise(fields[0], jnp.minimum(2 * step + 2, planes - 1))
    pair_sums(fields[3], weight, rows, there, here, planes + steps + step)

    @pl.when(step == steps - 1)
    def _():
        encode(there, exponents, code, [(g * steps, g * steps + steps) for g in range(4)])


def edge_kernel(components, side, n_halos, halo_of, bins, table, where, along_x, along_y, along_z, own, other, *refs):
    count = len(components)
    halos, refs = refs[:n_halos], refs[n_halos:]
    code, here, there, exponents, weight = refs[:5]
    fields, crosses, (u_full, sems) = refs[5:7], refs[7 : 7 + count], refs[7 + count :]
    rows, pair = u_full.shape[3], fields[0].shape[1]
    pairs = []
    for g, source in enumerate((own, other)):
        for p in range(2):
            pairs.append((source.at[:, 0, where[side + EDGE] + p], u_full.at[g, p]))
        for c, cross in zip(components, crosses):
            for p in range(4):
                for b in range(2):
                    lane = lanes_from((where[side + OWN_AT] + p) * pair + b * 128, 128)
                    plane = source.at[:, c, where[side + OWN] + p, :, block_of(where, b)]
                    pairs.append((plane, cross.at[g, :, :, lane]))
            for p in range(2):
                lane = lanes_from((where[side + HALO_AT] + p) * pair, pair)
                pairs.append((halo_of(halos, g).at[:, c - components[0], p], cross.at[g, :, :, lane]))
    run_copies(pairs, sems, lambda: spread_weights(bins, table, weight))

    def fill(n):
        i, p = n // 2, n % 2
        planes = crosses[i][:, :, :, pl.ds(p * pair, 5 * pair)]
        if components[i] == 2:
            fill_y(fields[n % 2], along_x, along_z, u_full[:, p], planes)
        else:
            halves = jnp.concatenate([u_full[:, p, :, :, block_of(where, b)] for b in range(2)], axis=-1)
            fill_z(fields[n % 2], along_x, along_y, halves, planes)

    fill(0)
    for n in range(2 * count):
        if n + 1 < 2 * count:
            fill(n + 1)
        pair_sums(fields[n % 2], weight, rows, there, here, n)
    encode(there, exponents, code, [(2 * i, 2 * i + 2) for i in range(count)])


def solve(inverse, here, code, scales, cells, group, store):
    start, stop = cells
    count, groups = here.shape[0], scales.shape[0] // 3
    depth = here.shape[1]
    sums = []
    for j in range(count):
        coded = code[j * depth + start : j * depth + stop].astype(jnp.int32).astype(jnp.float32)
        sums.append(here[j, start:stop] + coded * scales[j * groups + group : j * groups + group + 1, :])
    for i in range(3):
        store(i, inverse[3 * i] * sums[0] + inverse[3 * i + 1] * sums[1] + inverse[3 * i + 2] * sums[2])


def finish_kernel(inverse, here, code, exponents, out, scales):
    planes = out.shape[3]
    half = planes // 2

    @pl.when(pl.program_id(0) == 0)
    def _():
        decode_scales(exponents[...], scales)

    rows = scales.shape[0] // ORDERS
    own = scales.at[pl.ds(pl.program_id(0) * rows, rows)]
    for group in range(4):
        cells = group * half, group * half + half

        def store(i, value, group=group):
            if group < 2:
                out[i, 0, 0, group * half : group * half + half] = value
            else:
                out[i, group - 1, 0, 2 : planes - 2] = value

        solve(inverse, here.at[0], code, own, cells, group, store)


def finish_edges_kernel(bins, table, where, inverse, along_x, along_y, own, other, across, diagonal, halo, *refs):
    near, far_y, refs = refs[:2], refs[2:4], refs[4:]
    _, out, near_out, far_out, near_scales, far_scales, weight, *fields, u_half, v_half, sems, out_sems = refs
    parts, _, _, rows, width = u_half.shape
    pairs = []
    for g in range(parts):
        for p in range(2):
            if g < 2:
                u = (own, other)[g].at[:, 0, where[FAR + EDGE] + p, :, block_of(where, 1)]
            else:
                u = (across, diagonal)[g - 2].at[:, 4 + p]
            pairs.append((u, u_half.at[g, p]))
            lane = lanes_from((where[FAR + HALO_AT] + p) * width, width)
            pairs.append((halo.at[g, :, p], v_half.at[g, :, :, lane]))
        for p in range(4):
            if g < 2:
                v = (own, other)[g].at[:, 1, where[FAR + OWN] + p, :, block_of(where, 1)]
            else:
                v = (across, diagonal)[g - 2].at[:, p]
            lane = lanes_from((where[FAR + OWN_AT] + p) * width, width)
            pairs.append((v, v_half.at[g, :, :, lane]))
    run_copies(pairs, sems, lambda: spread_weights(bins, table, weight))

    for p in range(2):
        fill_z(fields[p], along_x, along_y, u_half[:, p], v_half[:, :, :, pl.ds(p * width, 5 * width)])
    decode_scales(near[1][ORDERS * 12 :], near_scales)
    decode_scales(far_y[1][ORDERS * 6 :], far_scales)
    for k in range(ORDERS):
        for c in range(2):
            def store_near(i, value, c=c, k=k):
                near_out[i, c, k] = value

            cells, scales = (2 - 2 * c, 4 - 2 * c), near_scales.at[pl.ds(6 * k, 6)]
            solve(inverse, near[0].at[k], near[1].at[pl.ds(12 * k, 12)], scales, cells, 1 - c, store_near)

        def store_far(i, value, k=k):
            far_out[i, 0, k] = value

        scales = far_scales.at[pl.ds(3 * k, 3)]
        solve(inverse, far_y[0].at[k], far_y[1].at[pl.ds(6 * k, 6)], scales, (0, 2), 0, store_far)
    for p in range(2):
        def store_sums(at, sums, p=p):
            for k in range(ORDERS):
                for i in range(3):
                    far_out[i, 1, k, p, at, :] = (
                        inverse[3 * i, at] * sums[0][k]
                        + inverse[3 * i + 1, at] * sums[1][k]
                        + inverse[3 * i + 2, at] * sums[2][k]
                    )

        power_sums(fields[p], weight, 0, rows, store_sums)
    run_copies(
        [
            (near_out, out.at[:, pl.ds(1, 2), :, pl.ds(where[NEAR + EDGE], 2)]),
            (far_out, out.at[:, pl.ds(1, 2), :, pl.ds(where[FAR + EDGE], 2)]),
        ],
        out_sems,
    )


def pack_near_kernel(where, own, near, sems):
    planes = pl.ds(where[NEAR + EDGE], 2)
    run_copies(
        [
            (own.at[:, pl.ds(1, 2), planes, :, block_of(where, b)], near.at[:, :, :, :, pl.ds(b * 128, 128)])
            for b in range(2)
        ],
        sems,
    )


def pack_across_kernel(where, own, across, diagonal, sems):
    pairs = []
    for target, b in ((across, 0), (diagonal, 2)):
        lane = block_of(where, b)
        pairs.append((own.at[:, 1, pl.ds(where[FAR + OWN], 4), :, lane], target.at[:, pl.ds(0, 4)]))
        pairs.append((own.at[:, 0, pl.ds(where[FAR + EDGE], 2), :, lane], target.at[:, pl.ds(4, 2)]))
    run_copies(pairs, sems)


def pack_other_kernel(where, own, other, near, far, sems):
    pairs = []
    for b in range(2):
        source, target = block_of(where, b), pl.ds(b * 128, 128)
        planes = pl.ds(where[NEAR + EDGE], 2)
        pairs.append((other.at[:, pl.ds(1, 2), planes, :, source], near.at[:, :, :, :, target]))
        planes = pl.ds(where[FAR + EDGE], 2)
        for g, array in enumerate((own, other)):
            pairs.append((array.at[:, pl.ds(2, 1), planes, :, source], far.at[g, :, :, :, :, target]))
    run_copies(pairs, sems)


def pack_far_kernel(where, own, other, across, diagonal, far, sems):
    planes = pl.ds(where[FAR + EDGE], 2)
    pairs = [(array.at[:, 1, planes, :, block_of(where, 1)], far.at[g]) for g, array in enumerate((own, other))]
    planes = pl.ds(where[FAR + EDGE_AT], 2)
    pairs += [(array.at[:, planes], far.at[2 + g]) for g, array in enumerate((across, diagonal))]
    run_copies(pairs, sems)


def smem():
    return pl.BlockSpec(memory_space=pltpu.SMEM)


def hbm():
    return pl.BlockSpec(memory_space=pl.ANY)


def vmem():
    return pl.BlockSpec(memory_space=pltpu.VMEM)


def after(value, *others):
    return lax.optimization_barrier((value, *others))[0]


def local(velocity, phase_bins):
    snaps, _, planes, rows, lanes = velocity.shape
    kind = velocity.dtype
    snap, slab = lax.axis_index("snap"), lax.axis_index("slab")
    n_snap, n_slab = lax.axis_size("snap"), lax.axis_size("slab")
    width = lanes // n_snap
    pair, size = 2 * width, snaps * rows
    odd = lax.rem(slab, 2)

    near_pairs = [(i, i ^ 1) for i in range(n_slab)]
    far_pairs = [(i, i + 1) for i in range(1, n_slab - 1, 2)]
    far_pairs = far_pairs + [(j, i) for i, j in far_pairs]
    core_pairs = [(i, i ^ 1) for i in range(n_snap)]
    chip_pairs = [(i, (i + 2) % n_snap) for i in range(n_snap)]
    diagonal_pairs = [(i, ((i + 2) % n_snap) ^ 1) for i in range(n_snap)]

    chip, core = lax.div(snap, 2), lax.rem(snap, 2)
    there, here = (1 - chip) * 2, chip * 2
    entries = [there + core, here + core, there + 1 - core]
    for high in (1 - odd, odd):
        entries += [high * (planes - 2), high * (planes - 4), 2 - high * 2, high * 4, high * 2]
    where = jnp.stack([jnp.asarray(entry, jnp.int32) for entry in entries])

    def pack(kernel, arrays, shapes, copies):
        return pl.pallas_call(
            kernel,
            in_specs=[smem()] + [hbm()] * len(arrays),
            out_specs=[vmem()] * len(shapes),
            out_shape=[jax.ShapeDtypeStruct(shape, kind) for shape in shapes],
            scratch_shapes=[pltpu.SemaphoreType.DMA((copies,))],
            **PARAMS,
        )(where, *arrays)

    near_shape, far_shape = (snaps, 2, 2, rows, pair), (2, snaps, 1, 2, rows, pair)
    table = jnp.asarray(phase_table().reshape(-1))
    along_x = jnp.asarray(five_planes(pair), jnp.bfloat16)
    along_x_half = jnp.asarray(five_planes(width), jnp.bfloat16)
    along_y = jnp.asarray(np.kron(np.eye(snaps, dtype=np.float32), band(rows)), jnp.bfloat16)
    along_z = jnp.asarray(band(lanes).T, jnp.bfloat16)
    along_z = jnp.concatenate(
        [lax.dynamic_slice_in_dim(along_z, where[b] * width, width, axis=1) for b in range(2)], axis=1
    )
    weight = pltpu.VMEM((2 * snaps, 2, 8, 128), jnp.float32)
    field = pltpu.VMEM((2 * size, pair), jnp.float32)

    def sums(cells, groups):
        shape = (ORDERS, 3, cells, rows, width)
        last = -(-ORDERS * 3 * groups // rows)
        return {
            "in_specs": [smem()] * 3 + [vmem()] * 3 + [hbm()] * 2,
            "out_shape": [
                jax.ShapeDtypeStruct((ORDERS * 3 * cells + last, rows, width), jnp.int16),
                jax.ShapeDtypeStruct(shape, jnp.float32),
            ],
            "out_specs": [vmem()] * 2,
            **PARAMS,
        }, [pltpu.VMEM(shape, jnp.float32), pltpu.VMEM((last * rows, width), jnp.float32), weight]

    def inside_sums(bins):
        steps = planes // 2
        call, scratch = sums(2 * planes, 4)
        return pl.pallas_call(
            inside_kernel,
            grid=(steps,),
            scratch_shapes=[
                *scratch, field, field, field, field,
                pltpu.VMEM((2, steps, snaps, rows, lanes), kind),
                pltpu.VMEM((2, planes, snaps, rows, lanes), kind),
                pltpu.VMEM((2, snaps, rows, planes * pair), kind),
                pltpu.VMEM((2, snaps, rows, planes * pair), kind),
                pltpu.SemaphoreType.DMA((planes, 12)),
            ],
            **call,
        )(bins, table, where, along_x, along_y, along_z, velocity, other)

    def edge_sums(bins, components, side, halos, halo_of):
        count = len(components)

        def body(*refs):
            edge_kernel(components, side, len(halos), halo_of, *refs)

        call, scratch = sums(2 * count, count)
        call["in_specs"] = call["in_specs"] + [hbm()] * len(halos)
        return pl.pallas_call(
            body,
            scratch_shapes=[
                *scratch, field, field,
                *[pltpu.VMEM((2, snaps, rows, 6 * pair), kind)] * count,
                pltpu.VMEM((2, 2, snaps, rows, lanes), kind),
                pltpu.SemaphoreType.DMA((4 + 20 * count,)),
            ],
            **call,
        )(bins, table, where, along_x, along_y, along_z, velocity, other, *halos)

    def exchange(parts):
        code, here = parts
        return here, lax.ppermute(code, "snap", chip_pairs)

    other = lax.ppermute(velocity, "snap", core_pairs)
    pair_bins = jnp.concatenate([phase_bins, lax.ppermute(phase_bins, "snap", core_pairs)])
    with jax.named_scope("pack"):
        (near_own,) = pack(pack_near_kernel, (velocity,), [near_shape], 2)
        halo_own = lax.ppermute(near_own, "slab", near_pairs)
        for_across, for_diagonal = pack(
            pack_across_kernel, (after(velocity, near_own),), [(snaps, 6, rows, width)] * 2, 4
        )
        across = lax.ppermute(for_across, "snap", chip_pairs)
        diagonal = lax.ppermute(for_diagonal, "snap", diagonal_pairs)
        near_other, far_w = pack(
            pack_other_kernel, (velocity, after(other, for_across, for_diagonal)), [near_shape, far_shape], 6
        )
        halo_other = lax.ppermute(near_other, "slab", near_pairs)

    with jax.named_scope("inside"):
        inside_parts = inside_sums(after(pair_bins, near_other, far_w))
        inside = exchange(inside_parts)

    with jax.named_scope("pack"):
        (far_v,) = pack(
            pack_far_kernel, (velocity, after(other, inside_parts[0]), across, diagonal), [(4, snaps, 2, rows, width)], 4
        )
    halo_w = lax.ppermute(after(far_w, halo_other, halo_own, inside_parts[0]), "slab", far_pairs)
    halo_v = lax.ppermute(after(far_v, halo_other, halo_own), "slab", far_pairs)

    with jax.named_scope("edge_near"):
        near = exchange(edge_sums(pair_bins, (1, 2), NEAR, (halo_own, halo_other), lambda halos, g: halos[g]))
    with jax.named_scope("edge_far"):
        ready = after(pair_bins, inside[1])
        far_y = exchange(edge_sums(ready, (2,), FAR, (halo_w,), lambda halos, g: halos[0].at[g]))

    all_bins = jnp.concatenate([pair_bins, lax.ppermute(pair_bins, "snap", chip_pairs)])
    with jax.named_scope("invert"):
        inverse = pl.pallas_call(
            invert_kernel,
            in_specs=[smem(), smem()],
            out_shape=jax.ShapeDtypeStruct((9, rows, width), jnp.float32),
            **PARAMS,
        )(all_bins, table)

    out_shape = jax.ShapeDtypeStruct((3, 3, ORDERS, planes, rows, width), jnp.float32)

    last = 3
    with jax.named_scope("finish"):
        out = pl.pallas_call(
            finish_kernel,
            out_shape=out_shape,
            grid=(ORDERS,),
            in_specs=[
                pl.BlockSpec((9, rows, width), lambda p: (0, 0, 0)),
                pl.BlockSpec((1, 3, 2 * planes, rows, width), lambda p: (p, 0, 0, 0, 0)),
                pl.BlockSpec((6 * planes, rows, width), lambda p: (p, 0, 0)),
                pl.BlockSpec((last, rows, width), lambda p: (ORDERS * 6 * planes // last, 0, 0)),
            ],
            out_specs=pl.BlockSpec((3, 3, 1, planes, rows, width), lambda p: (0, 0, p, 0, 0, 0)),
            scratch_shapes=[pltpu.VMEM((last * rows, width), jnp.float32)],
            **PARAMS,
        )(inverse, *inside, inside[1])

    with jax.named_scope("finish_edges"):
        edges = pltpu.VMEM((3, 2, ORDERS, 2, rows, width), jnp.float32)
        return pl.pallas_call(
            finish_edges_kernel,
            out_shape=out_shape,
            in_specs=[smem()] * 3 + [vmem()] * 3 + [hbm()] * 5 + [vmem()] * 4 + [hbm()],
            out_specs=hbm(),
            scratch_shapes=[
                edges, edges,
                pltpu.VMEM((2 * rows, width), jnp.float32),
                pltpu.VMEM((rows, width), jnp.float32),
                pltpu.VMEM((4 * snaps, 2, 8, 128), jnp.float32),
                pltpu.VMEM((4 * size, width), jnp.float32),
                pltpu.VMEM((4 * size, width), jnp.float32),
                pltpu.VMEM((4, 2, snaps, rows, width), kind),
                pltpu.VMEM((4, snaps, rows, 6 * width), kind),
                pltpu.SemaphoreType.DMA((32,)),
                pltpu.SemaphoreType.DMA((2,)),
            ],
            input_output_aliases={15: 0},
            **PARAMS,
        )(
            all_bins, table, where, inverse, along_x_half, along_y, velocity, other, across, diagonal,
            after(halo_v, out), *near, *far_y, out,
        )


def solution(mesh):
    in_specs = (P("snap", None, "slab", None, None), P("snap"))
    out_specs = P(None, None, None, "slab", None, "snap")
    return jax.shard_map(local, mesh=mesh, in_specs=in_specs, out_specs=out_specs, check_vma=False)
```

```python
import jax
import jax.numpy as jnp
import numpy as np
from jax import lax
from jax.experimental import pallas as pl
from jax.experimental.pallas import tpu as pltpu
from jax.sharding import PartitionSpec as P

BINS = 180
ORDERS = 4
TAPS = ((-2, 1.0), (-1, -8.0), (1, 8.0), (2, -1.0))
STEP = 0.75 / 12.0
LEVELS = 32766.0
TINY = 1e-30


def band(size):
    matrix = np.zeros((size, size), np.float32)
    for offset, factor in TAPS:
        matrix += factor * np.eye(size, k=offset, dtype=np.float32)
    return matrix


def four_planes(width):
    return np.concatenate([factor * np.eye(width, dtype=np.float32) for _, factor in TAPS])


def phase_table():
    centers = (np.arange(BINS, dtype=np.float32) + np.float32(0.5)) * np.float32(2.0 * np.pi / BINS)
    return np.stack([np.cos(centers), np.sin(centers)], axis=1).astype(np.float32)


def weights_kernel(bins, table, weight):
    for s in range(bins.shape[0]):
        weight[s, 0] = jnp.full(weight.shape[2:], table[bins[s] * 2], jnp.float32)
        weight[s, 1] = jnp.full(weight.shape[2:], table[bins[s] * 2 + 1], jnp.float32)


def invert_kernel(weight, inverse):
    g01 = g02 = g11 = g12 = g22 = jnp.zeros(weight.shape[2:], jnp.float32)
    for s in range(weight.shape[0]):
        cosine, sine = weight[s, 0], weight[s, 1]
        g01, g02 = g01 + cosine, g02 + sine
        g11, g12, g22 = g11 + cosine * cosine, g12 + cosine * sine, g22 + sine * sine
    g00 = jnp.full(weight.shape[2:], weight.shape[0], jnp.float32)
    c00 = g11 * g22 - g12 * g12
    c01 = g02 * g12 - g01 * g22
    c02 = g01 * g12 - g02 * g11
    c11 = g00 * g22 - g02 * g02
    c12 = g02 * g01 - g00 * g12
    c22 = g00 * g11 - g01 * g01
    determinant = g00 * c00 + g01 * c01 + g02 * c02
    for i, entry in enumerate((c00, c01, c02, c01, c11, c12, c02, c12, c22)):
        for half in range(inverse.shape[1] // 8):
            inverse[i, pl.ds(half * 8, 8)] = entry / determinant


class Spot:
    def __init__(self, planes):
        snap, odd = lax.axis_index("snap"), lax.rem(lax.axis_index("slab"), 2)
        chip, core = lax.div(snap, 2), lax.rem(snap, 2)
        there, here = (1 - chip) * 2, chip * 2
        self.there, self.here, self.diagonal = there + core, here + core, there + 1 - core
        self.near, self.far = Side(planes, 1 - odd), Side(planes, odd)

    def lanes(self, block):
        return lanes_from(block * 128, 128)

    def pair(self):
        return self.lanes(self.there), self.lanes(self.here)


class Side:
    def __init__(self, planes, high):
        self.high = high == 1
        self.edge, self.own, self.own_at = high * (planes - 2), high * (planes - 4), 2 - high * 2
        self.halo_at, self.edge_at = high * 4, high * 2

    def around(self, p, own, halo):
        planes = []
        for offset, _ in TAPS:
            at = p + 2 + offset
            if at < 2:
                planes.append(jnp.where(self.high, own(at), halo(at)))
            elif at < 4:
                planes.append(own(at - self.own_at))
            else:
                planes.append(jnp.where(self.high, halo(at - 4), own(at - 2)))
        return jnp.concatenate(planes, axis=1)


def lanes_from(start, size):
    return pl.ds(pl.multiple_of(start, 128), size)


def power_sums(field, weight, lane, half, rows, store):
    total = [None] * (3 * ORDERS)
    for s in range(weight.shape[0]):
        first = field[pl.ds(s * rows + half * 8, 8), pl.ds(lane, 128)]
        second = first * first
        powers = (first, second, second * first, second * second)
        for j in range(3):
            for k in range(ORDERS):
                term = powers[k] if j == 0 else powers[k] * weight[s, j - 1]
                at = j * ORDERS + k
                total[at] = term if s == 0 else total[at] + term
    store(pl.ds(half * 8, 8), [[total[j * ORDERS + k] * STEP ** (k + 1) for k in range(ORDERS)] for j in range(3)])


def pair_sums(field, weight, rows, there, here, cell):
    def piece(half, lane, target):
        def store(at, sums):
            for j in range(3):
                for k in range(ORDERS):
                    target[k, j, cell, at, :] = sums[j][k]

        power_sums(field, weight, lane, half, rows, store)

    return [
        lambda half=half, lane=lane, target=target: piece(half, lane, target)
        for lane, target in ((0, there), (128, here))
        for half in range(rows // 8)
    ]


def weave(pieces, chunks):
    done = 0
    for i, piece in enumerate(pieces):
        piece()
        while done * len(pieces) < (i + 1) * len(chunks):
            chunks[done]()
            done += 1


def encode(sums, exponents, code, groups):
    cells, rows = sums.shape[2:4]
    exponents[...] = jnp.zeros(exponents.shape, jnp.float32)
    for n in range(ORDERS * 3):
        for g, (start, stop) in enumerate(groups):
            value = sums[n // 3, n % 3, start:stop]
            top = jnp.max(jnp.max(jnp.abs(value), axis=0), axis=0, keepdims=True)
            exponent = jnp.ceil(jnp.log(jnp.maximum(top, TINY)) * np.float32(1.0 / np.log(2.0)))
            rounded = jnp.round(value * (jnp.exp2(-exponent) * LEVELS))
            code[n * cells + start : n * cells + stop] = rounded.astype(jnp.int32).astype(jnp.int16)
            exponents[pl.ds(n * len(groups) + g, 1), :] = exponent
    last = exponents[...].reshape(exponents.shape[0] // rows, rows, exponents.shape[1])
    code[ORDERS * 3 * cells :] = last.astype(jnp.int32).astype(jnp.int16)


def decode_scales(code, scales):
    exponents = code.astype(jnp.int32).astype(jnp.float32)
    scales[...] = (jnp.exp2(exponents) * (1.0 / LEVELS)).reshape(scales.shape)


def flat(block):
    return block.reshape(block.shape[0] * block.shape[1], block.shape[2])


def product(a, b):
    return jnp.dot(a, b, preferred_element_type=jnp.float32)


def make_copies(pairs, sems):
    return [pltpu.make_async_copy(source, target, sems.at[i]) for i, (source, target) in enumerate(pairs)]


def run_copies(pairs, sems):
    copies = make_copies(pairs, sems)
    for copy in copies:
        copy.start()
    for copy in copies:
        copy.wait()


def fill_x(field, along_y, along_z, v, w):
    size = along_y.shape[0]

    def chunk(g):
        field[pl.ds(g * size, size), :] = product(along_y[...], w(g)) - product(v(g), along_z())

    return [lambda g=g: chunk(g) for g in range(field.shape[0] // size)]


def fill_y(field, along_x, along_y, along_z, u, planes):
    size = along_y.shape[0]

    def chunk(g):
        field[pl.ds(g * size, size), :] = product(u(g), along_z()) - product(planes(g), along_x[...])

    return [lambda g=g: chunk(g) for g in range(field.shape[0] // size)]


def fill_z(field, along_x, along_y, u, planes):
    size = along_y.shape[0]

    def chunk(g):
        field[pl.ds(g * size, size), :] = product(planes(g), along_x[...]) - product(along_y[...], u(g))

    return [lambda g=g: chunk(g) for g in range(field.shape[0] // size)]


def run(chunks):
    for chunk in chunks:
        chunk()


def halves(spot, load):
    return jnp.concatenate([flat(load(block)) for block in spot.pair()], axis=1)


def inside_kernel(weight, along_x, along_y, all_z, own, other, code, here, there, exponents, *fields):
    planes, rows = own.shape[2:4]
    steps = planes // 2
    spot = Spot(planes)
    sources = (own, other)

    def half(c, g, p):
        return halves(spot, lambda block: sources[g][:, c, p, :, block])

    def along_z():
        return jnp.concatenate([all_z[:, block] for block in spot.pair()], axis=1)

    def streamwise(field, p):
        return fill_x(field, along_y, along_z, lambda g: flat(sources[g][:, 1, p]), lambda g: half(2, g, p))

    def around(c, g, p):
        return jnp.concatenate([half(c, g, p + offset) for offset, _ in TAPS], axis=1)

    def summed(i, cell):
        return pair_sums(fields[i], weight, rows, there, here, cell)

    run(streamwise(fields[0], 0))

    @pl.loop(0, steps)
    def _(step):
        p = step + 2
        weave(summed(0, 2 * step), streamwise(fields[1], 2 * step + 1))
        weave(
            summed(1, 2 * step + 1),
            fill_z(fields[3], along_x, along_y, lambda g: half(0, g, p), lambda g: around(1, g, p)),
        )
        weave(
            summed(3, planes + steps + step),
            fill_y(
                fields[2], along_x, along_y, along_z,
                lambda g: flat(sources[g][:, 0, p]), lambda g: around(2, g, p),
            ),
        )
        weave(summed(2, planes + step), streamwise(fields[0], jnp.minimum(2 * step + 2, planes - 1)))

    encode(there, exponents, code, [(g * steps, g * steps + steps) for g in range(4)])


def edge_kernel(components, near, n_halos, halo_of, weight, along_x, along_y, all_z, own, other, *refs):
    count = len(components)
    halos, (code, here, there, exponents, *fields) = refs[:n_halos], refs[n_halos:]
    rows = own.shape[3]
    spot = Spot(own.shape[2])
    side = spot.near if near else spot.far
    sources = (own, other)

    def along_z():
        return jnp.concatenate([all_z[:, block] for block in spot.pair()], axis=1)

    def fill(n):
        c, p = components[n // 2], n % 2

        def around(g):
            return side.around(
                p,
                lambda i: halves(spot, lambda block: sources[g][:, c, side.own + i, :, block]),
                lambda i: flat(halo_of(halos, g)[:, c - components[0], i]),
            )

        if c == 2:
            return fill_y(
                fields[n % 2], along_x, along_y, along_z, lambda g: flat(sources[g][:, 0, side.edge + p]), around
            )
        return fill_z(
            fields[n % 2], along_x, along_y,
            lambda g: halves(spot, lambda block: sources[g][:, 0, side.edge + p, :, block]), around,
        )

    run(fill(0))
    for n in range(2 * count):
        weave(
            pair_sums(fields[n % 2], weight, rows, there, here, n),
            fill(n + 1) if n + 1 < 2 * count else [],
        )
    encode(there, exponents, code, [(2 * i, 2 * i + 2) for i in range(count)])


def solve(inverse, here, code, scales, cells, group, store):
    start, stop = cells
    count, groups = here.shape[0], scales.shape[0] // 3
    depth = here.shape[1]
    sums = []
    for j in range(count):
        coded = code[j * depth + start : j * depth + stop].astype(jnp.int32).astype(jnp.float32)
        sums.append(here[j, start:stop] + coded * scales[j * groups + group : j * groups + group + 1, :])
    for i in range(3):
        store(i, inverse[3 * i] * sums[0] + inverse[3 * i + 1] * sums[1] + inverse[3 * i + 2] * sums[2])


def finish_kernel(inverse, here, code, exponents, out, scales):
    planes = out.shape[3]
    half = planes // 2

    @pl.when(pl.program_id(0) == 0)
    def _():
        decode_scales(exponents[...], scales)

    rows = scales.shape[0] // ORDERS
    own = scales.at[pl.ds(pl.program_id(0) * rows, rows)]
    for group in range(4):
        cells = group * half, group * half + half

        def store(i, value, group=group):
            if group < 2:
                out[i, 0, 0, group * half : group * half + half] = value
            else:
                out[i, group - 1, 0, 2 : planes - 2] = value

        solve(inverse, here.at[0], code, own, cells, group, store)


def finish_edges_kernel(weight, inverse, along_x, along_y, own, other, across, diagonal, halo, *refs):
    near_here, near_code, far_here, far_code, _, out, near_out, far_out = refs[:8]
    near_scales, far_scales, *fields, out_sems = refs[8:]
    rows = own.shape[3]
    spot = Spot(own.shape[2])
    side, lane_here = spot.far, spot.lanes(spot.here)
    sources = (own, other, across, diagonal)

    def fill(p):
        def u(g):
            return flat(sources[g][:, 0, side.edge + p, :, lane_here] if g < 2 else sources[g][:, 4 + p])

        def own_plane(g, i):
            return flat(sources[g][:, 1, side.own + i, :, lane_here] if g < 2 else sources[g][:, i])

        def around(g):
            return side.around(p, lambda i: own_plane(g, i), lambda i: flat(halo[g, :, i]))

        return fill_z(fields[p], along_x, along_y, u, around)

    def solve_order(k):
        for c in range(2):
            def store_near(i, value, c=c):
                near_out[i, c, k] = value

            cells, scales = (2 - 2 * c, 4 - 2 * c), near_scales.at[pl.ds(6 * k, 6)]
            solve(inverse, near_here.at[k], near_code.at[pl.ds(12 * k, 12)], scales, cells, 1 - c, store_near)

        def store_far(i, value):
            far_out[i, 0, k] = value

        scales = far_scales.at[pl.ds(3 * k, 3)]
        solve(inverse, far_here.at[k], far_code.at[pl.ds(6 * k, 6)], scales, (0, 2), 0, store_far)

    def sum_half(p, half):
        def store(at, sums):
            for k in range(ORDERS):
                for i in range(3):
                    far_out[i, 1, k, p, at, :] = (
                        inverse[3 * i, at] * sums[0][k]
                        + inverse[3 * i + 1, at] * sums[1][k]
                        + inverse[3 * i + 2, at] * sums[2][k]
                    )

        power_sums(fields[p], weight, 0, half, rows, store)

    decode_scales(near_code[ORDERS * 12 :], near_scales)
    decode_scales(far_code[ORDERS * 6 :], far_scales)
    weave([lambda k=k: solve_order(k) for k in range(ORDERS)], fill(0))
    near_copy, far_copy = make_copies(
        [
            (near_out, out.at[:, pl.ds(1, 2), :, pl.ds(spot.near.edge, 2)]),
            (far_out, out.at[:, pl.ds(1, 2), :, pl.ds(spot.far.edge, 2)]),
        ],
        out_sems,
    )
    near_copy.start()
    weave([lambda half=half: sum_half(0, half) for half in range(rows // 8)], fill(1))
    for half in range(rows // 8):
        sum_half(1, half)
    far_copy.start()
    near_copy.wait()
    far_copy.wait()


def pack_near_kernel(own, near, sems):
    spot = Spot(own.shape[2])
    planes = pl.ds(spot.near.edge, 2)
    run_copies(
        [
            (own.at[:, pl.ds(1, 2), planes, :, block], near.at[:, :, :, :, pl.ds(b * 128, 128)])
            for b, block in enumerate(spot.pair())
        ],
        sems,
    )


def pack_across_kernel(own, across, diagonal, sems):
    spot = Spot(own.shape[2])
    pairs = []
    for target, block in ((across, spot.there), (diagonal, spot.diagonal)):
        lane = spot.lanes(block)
        pairs.append((own.at[:, 1, pl.ds(spot.far.own, 4), :, lane], target.at[:, pl.ds(0, 4)]))
        pairs.append((own.at[:, 0, pl.ds(spot.far.edge, 2), :, lane], target.at[:, pl.ds(4, 2)]))
    run_copies(pairs, sems)


def pack_other_kernel(own, other, near, far, sems):
    spot = Spot(own.shape[2])
    pairs = []
    for b, source in enumerate(spot.pair()):
        target = pl.ds(b * 128, 128)
        planes = pl.ds(spot.near.edge, 2)
        pairs.append((other.at[:, pl.ds(1, 2), planes, :, source], near.at[:, :, :, :, target]))
        planes = pl.ds(spot.far.edge, 2)
        for g, array in enumerate((own, other)):
            pairs.append((array.at[:, pl.ds(2, 1), planes, :, source], far.at[g, :, :, :, :, target]))
    run_copies(pairs, sems)


def pack_far_kernel(own, other, across, diagonal, far, sems):
    spot = Spot(own.shape[2])
    planes, lane = pl.ds(spot.far.edge, 2), spot.lanes(spot.here)
    pairs = [(array.at[:, 1, planes, :, lane], far.at[g]) for g, array in enumerate((own, other))]
    planes = pl.ds(spot.far.edge_at, 2)
    pairs += [(array.at[:, planes], far.at[2 + g]) for g, array in enumerate((across, diagonal))]
    run_copies(pairs, sems)


def params(megabytes):
    return {
        "compiler_params": pltpu.CompilerParams(vmem_limit_bytes=megabytes * 2**20),
        "cost_estimate": pl.CostEstimate(flops=1, bytes_accessed=1, transcendentals=0),
    }


def smem():
    return pl.BlockSpec(memory_space=pltpu.SMEM)


def hbm():
    return pl.BlockSpec(memory_space=pl.ANY)


def vmem():
    return pl.BlockSpec(memory_space=pltpu.VMEM)


def after(value, *others):
    return lax.optimization_barrier((value, *others))[0]


def local(velocity, phase_bins):
    snaps, _, planes, rows, lanes = velocity.shape
    kind = velocity.dtype
    n_snap, n_slab = lax.axis_size("snap"), lax.axis_size("slab")
    width = lanes // n_snap
    pair, size = 2 * width, snaps * rows

    near_pairs = [(i, i ^ 1) for i in range(n_slab)]
    far_pairs = [(i, i + 1) for i in range(1, n_slab - 1, 2)]
    far_pairs = far_pairs + [(j, i) for i, j in far_pairs]
    core_pairs = [(i, i ^ 1) for i in range(n_snap)]
    chip_pairs = [(i, (i + 2) % n_snap) for i in range(n_snap)]
    diagonal_pairs = [(i, ((i + 2) % n_snap) ^ 1) for i in range(n_snap)]

    def pack(kernel, arrays, shapes, copies):
        return pl.pallas_call(
            kernel,
            in_specs=[hbm()] * len(arrays),
            out_specs=[vmem()] * len(shapes),
            out_shape=[jax.ShapeDtypeStruct(shape, kind) for shape in shapes],
            scratch_shapes=[pltpu.SemaphoreType.DMA((copies,))],
            **params(8),
        )(*arrays)

    near_shape, far_shape = (snaps, 2, 2, rows, pair), (2, snaps, 1, 2, rows, pair)
    table = jnp.asarray(phase_table().reshape(-1))
    along_x = jnp.asarray(four_planes(pair), jnp.bfloat16)
    along_x_half = jnp.asarray(four_planes(width), jnp.bfloat16)
    along_y = jnp.asarray(np.kron(np.eye(snaps, dtype=np.float32), band(rows)), jnp.bfloat16)
    along_z = jnp.asarray(band(lanes).T, jnp.bfloat16)
    field = pltpu.VMEM((2 * size, pair), jnp.float32)

    def sums(cells, groups):
        shape = (ORDERS, 3, cells, rows, width)
        last = -(-ORDERS * 3 * groups // rows)
        return {
            "out_shape": [
                jax.ShapeDtypeStruct((ORDERS * 3 * cells + last, rows, width), jnp.int16),
                jax.ShapeDtypeStruct(shape, jnp.float32),
            ],
        }, [pltpu.VMEM(shape, jnp.float32), pltpu.VMEM((last * rows, width), jnp.float32)]

    def inside_sums(weights):
        call, scratch = sums(2 * planes, 4)
        return pl.pallas_call(
            inside_kernel, scratch_shapes=[*scratch, field, field, field, field], **call, **params(26)
        )(weights, along_x, along_y, along_z, velocity, other)

    def edge_sums(weights, components, near, halos, halo_of):
        count = len(components)

        def body(*refs):
            edge_kernel(components, near, len(halos), halo_of, *refs)

        call, scratch = sums(2 * count, count)
        return pl.pallas_call(body, scratch_shapes=[*scratch, field, field], **call, **params(26))(
            weights, along_x, along_y, along_z, velocity, other, *halos
        )

    def exchange(parts):
        code, here = parts
        return here, lax.ppermute(code, "snap", chip_pairs)

    other = lax.ppermute(velocity, "snap", core_pairs)
    with jax.named_scope("pack"):
        (near_own,) = pack(pack_near_kernel, (velocity,), [near_shape], 2)
        halo_own = lax.ppermute(near_own, "slab", near_pairs)
    pair_bins = jnp.concatenate([phase_bins, lax.ppermute(phase_bins, "snap", core_pairs)])
    chip_bins = [lax.ppermute(phase_bins, "snap", pairs) for pairs in (chip_pairs, diagonal_pairs)]
    all_bins = jnp.concatenate([pair_bins, *chip_bins])

    def spread(bins):
        return pl.pallas_call(
            weights_kernel,
            in_specs=[smem(), smem()],
            out_shape=jax.ShapeDtypeStruct((bins.shape[0], 2, 8, 128), jnp.float32),
            **params(8),
        )(bins, table)

    with jax.named_scope("weights"):
        pair_weights = spread(pair_bins)
    with jax.named_scope("pack"):
        for_across, for_diagonal = pack(
            pack_across_kernel, (after(velocity, near_own),), [(snaps, 6, rows, width)] * 2, 4
        )
        across = lax.ppermute(for_across, "snap", chip_pairs)
        diagonal = lax.ppermute(for_diagonal, "snap", diagonal_pairs)
        near_other, far_w = pack(
            pack_other_kernel, (velocity, after(other, for_across, for_diagonal)), [near_shape, far_shape], 6
        )
        halo_other = lax.ppermute(near_other, "slab", near_pairs)

    with jax.named_scope("inside"):
        inside_parts = inside_sums(after(pair_weights, near_other, far_w))

    with jax.named_scope("pack"):
        (far_v,) = pack(
            pack_far_kernel, (velocity, after(other, inside_parts[0]), across, diagonal), [(4, snaps, 2, rows, width)], 4
        )
    inside = exchange((after(inside_parts[0], far_v), inside_parts[1]))
    halo_w = lax.ppermute(after(far_w, halo_other, halo_own, inside_parts[0]), "slab", far_pairs)
    halo_v = lax.ppermute(far_v, "slab", far_pairs)

    with jax.named_scope("edge_near"):
        near = exchange(edge_sums(pair_weights, (1, 2), True, (halo_own, halo_other), lambda halos, g: halos[g]))
    with jax.named_scope("edge_far"):
        ready = after(pair_weights, inside[1])
        far_y = exchange(edge_sums(ready, (2,), False, (halo_w,), lambda halos, g: halos[0].at[g]))

    with jax.named_scope("invert"):
        weights = spread(after(all_bins, inside_parts[0]))
        inverse = pl.pallas_call(
            invert_kernel, out_shape=jax.ShapeDtypeStruct((9, rows, width), jnp.float32), **params(8)
        )(weights)

    out_shape = jax.ShapeDtypeStruct((3, 3, ORDERS, planes, rows, width), jnp.float32)

    last = 3
    with jax.named_scope("finish"):
        out = pl.pallas_call(
            finish_kernel,
            out_shape=out_shape,
            grid=(ORDERS,),
            in_specs=[
                pl.BlockSpec((9, rows, width), lambda p: (0, 0, 0)),
                pl.BlockSpec((1, 3, 2 * planes, rows, width), lambda p: (p, 0, 0, 0, 0)),
                pl.BlockSpec((6 * planes, rows, width), lambda p: (p, 0, 0)),
                pl.BlockSpec((last, rows, width), lambda p: (ORDERS * 6 * planes // last, 0, 0)),
            ],
            out_specs=pl.BlockSpec((3, 3, 1, planes, rows, width), lambda p: (0, 0, p, 0, 0, 0)),
            scratch_shapes=[pltpu.VMEM((last * rows, width), jnp.float32)],
            **params(16),
        )(inverse, *inside, inside[1])

    with jax.named_scope("finish_edges"):
        edges = pltpu.VMEM((3, 2, ORDERS, 2, rows, width), jnp.float32)
        return pl.pallas_call(
            finish_edges_kernel,
            out_shape=out_shape,
            in_specs=[vmem()] * 13 + [hbm()],
            out_specs=hbm(),
            scratch_shapes=[
                edges, edges,
                pltpu.VMEM((2 * rows, width), jnp.float32),
                pltpu.VMEM((rows, width), jnp.float32),
                pltpu.VMEM((4 * size, width), jnp.float32),
                pltpu.VMEM((4 * size, width), jnp.float32),
                pltpu.SemaphoreType.DMA((2,)),
            ],
            input_output_aliases={13: 0},
            **params(26),
        )(
            weights, inverse, along_x_half, along_y, velocity, other, across, diagonal,
            after(halo_v, out), *near, *far_y, out,
        )


def solution(mesh):
    in_specs = (P("snap", None, "slab", None, None), P("snap"))
    out_specs = P(None, None, None, "slab", None, "snap")
    return jax.shard_map(local, mesh=mesh, in_specs=in_specs, out_specs=out_specs, check_vma=False)
```

```python
import jax
import jax.numpy as jnp
import numpy as np
from jax import lax
from jax.experimental import pallas as pl
from jax.experimental.pallas import tpu as pltpu
from jax.sharding import PartitionSpec as P

BINS = 180
ORDERS = 4
TAPS = ((-2, 1.0), (-1, -8.0), (1, 8.0), (2, -1.0))
STEP = 0.75 / 12.0
LEVELS = 32766.0
TINY = 1e-30


def band(size):
    matrix = np.zeros((size, size), np.float32)
    for offset, factor in TAPS:
        matrix += factor * np.eye(size, k=offset, dtype=np.float32)
    return matrix


def four_planes(width):
    return np.concatenate([factor * np.eye(width, dtype=np.float32) for _, factor in TAPS])


def phase_table():
    centers = (np.arange(BINS, dtype=np.float32) + np.float32(0.5)) * np.float32(2.0 * np.pi / BINS)
    return np.stack([np.cos(centers), np.sin(centers)], axis=1).astype(np.float32)


def weights_kernel(bins, table, weight):
    for s in range(bins.shape[0]):
        weight[s, 0] = jnp.full(weight.shape[2:], table[bins[s] * 2], jnp.float32)
        weight[s, 1] = jnp.full(weight.shape[2:], table[bins[s] * 2 + 1], jnp.float32)


def invert_kernel(weight, inverse):
    g01 = g02 = g11 = g12 = g22 = jnp.zeros(weight.shape[2:], jnp.float32)
    for s in range(weight.shape[0]):
        cosine, sine = weight[s, 0], weight[s, 1]
        g01, g02 = g01 + cosine, g02 + sine
        g11, g12, g22 = g11 + cosine * cosine, g12 + cosine * sine, g22 + sine * sine
    g00 = jnp.full(weight.shape[2:], weight.shape[0], jnp.float32)
    c00 = g11 * g22 - g12 * g12
    c01 = g02 * g12 - g01 * g22
    c02 = g01 * g12 - g02 * g11
    c11 = g00 * g22 - g02 * g02
    c12 = g02 * g01 - g00 * g12
    c22 = g00 * g11 - g01 * g01
    determinant = g00 * c00 + g01 * c01 + g02 * c02
    for i, entry in enumerate((c00, c01, c02, c01, c11, c12, c02, c12, c22)):
        for half in range(inverse.shape[1] // 8):
            inverse[i, pl.ds(half * 8, 8)] = entry / determinant


class Spot:
    def __init__(self, planes):
        snap, odd = lax.axis_index("snap"), lax.rem(lax.axis_index("slab"), 2)
        chip, core = lax.div(snap, 2), lax.rem(snap, 2)
        there, here = (1 - chip) * 2, chip * 2
        self.there, self.here, self.diagonal = there + core, here + core, there + 1 - core
        self.near, self.far = Side(planes, 1 - odd), Side(planes, odd)

    def lanes(self, block):
        return lanes_from(block * 128, 128)

    def pair(self):
        return self.lanes(self.there), self.lanes(self.here)


class Side:
    def __init__(self, planes, high):
        self.high = high == 1
        self.edge, self.own, self.own_at = high * (planes - 2), high * (planes - 4), 2 - high * 2
        self.halo_at, self.edge_at = high * 4, high * 2

    def around(self, p, own, halo):
        planes = []
        for offset, _ in TAPS:
            at = p + 2 + offset
            if at < 2:
                planes.append(jnp.where(self.high, own(at), halo(at)))
            elif at < 4:
                planes.append(own(at - self.own_at))
            else:
                planes.append(jnp.where(self.high, halo(at - 4), own(at - 2)))
        return jnp.concatenate(planes, axis=1)


def lanes_from(start, size):
    return pl.ds(pl.multiple_of(start, 128), size)


def power_sums(field, weight, lane, half, rows, store):
    total = [None] * (3 * ORDERS)
    for s in range(weight.shape[0]):
        first = field[pl.ds(s * rows + half * 8, 8), pl.ds(lane, 128)]
        second = first * first
        powers = (first, second, second * first, second * second)
        for j in range(3):
            for k in range(ORDERS):
                term = powers[k] if j == 0 else powers[k] * weight[s, j - 1]
                at = j * ORDERS + k
                total[at] = term if s == 0 else total[at] + term
    store(pl.ds(half * 8, 8), [[total[j * ORDERS + k] * STEP ** (k + 1) for k in range(ORDERS)] for j in range(3)])


def pair_sums(field, weight, rows, there, here, cell):
    def piece(half, lane, target):
        def store(at, sums):
            for j in range(3):
                for k in range(ORDERS):
                    target[k, j, cell, at, :] = sums[j][k]

        power_sums(field, weight, lane, half, rows, store)

    return [
        lambda half=half, lane=lane, target=target: piece(half, lane, target)
        for lane, target in ((0, there), (128, here))
        for half in range(rows // 8)
    ]


def weave(pieces, chunks):
    done = 0
    for i, piece in enumerate(pieces):
        piece()
        while done * len(pieces) < (i + 1) * len(chunks):
            chunks[done]()
            done += 1


def encode(sums, exponents, code, groups):
    cells, rows = sums.shape[2:4]
    exponents[...] = jnp.zeros(exponents.shape, jnp.float32)
    for n in range(ORDERS * 3):
        for g, (start, stop) in enumerate(groups):
            value = sums[n // 3, n % 3, start:stop]
            top = jnp.max(jnp.max(jnp.abs(value), axis=0), axis=0, keepdims=True)
            exponent = jnp.ceil(jnp.log(jnp.maximum(top, TINY)) * np.float32(1.0 / np.log(2.0)))
            rounded = jnp.round(value * (jnp.exp2(-exponent) * LEVELS))
            code[n * cells + start : n * cells + stop] = rounded.astype(jnp.int32).astype(jnp.int16)
            exponents[pl.ds(n * len(groups) + g, 1), :] = exponent
    last = exponents[...].reshape(exponents.shape[0] // rows, rows, exponents.shape[1])
    code[ORDERS * 3 * cells :] = last.astype(jnp.int32).astype(jnp.int16)


def decode_scales(code, scales):
    exponents = code.astype(jnp.int32).astype(jnp.float32)
    scales[...] = (jnp.exp2(exponents) * (1.0 / LEVELS)).reshape(scales.shape)


def flat(block):
    return block.reshape(block.shape[0] * block.shape[1], block.shape[2])


def product(a, b):
    return jnp.dot(a, b, preferred_element_type=jnp.float32)


def make_copies(pairs, sems):
    return [pltpu.make_async_copy(source, target, sems.at[i]) for i, (source, target) in enumerate(pairs)]


def run_copies(pairs, sems):
    copies = make_copies(pairs, sems)
    for copy in copies:
        copy.start()
    for copy in copies:
        copy.wait()


def fill_x(field, along_y, along_z, v, w):
    size = along_y.shape[0]

    def chunk(g):
        field[pl.ds(g * size, size), :] = product(along_y[...], w(g)) - product(v(g), along_z())

    return [lambda g=g: chunk(g) for g in range(field.shape[0] // size)]


def fill_y(field, along_x, along_y, along_z, u, planes):
    size = along_y.shape[0]

    def chunk(g):
        field[pl.ds(g * size, size), :] = product(u(g), along_z()) - product(planes(g), along_x[...])

    return [lambda g=g: chunk(g) for g in range(field.shape[0] // size)]


def fill_z(field, along_x, along_y, u, planes):
    size = along_y.shape[0]

    def chunk(g):
        field[pl.ds(g * size, size), :] = product(planes(g), along_x[...]) - product(along_y[...], u(g))

    return [lambda g=g: chunk(g) for g in range(field.shape[0] // size)]


def run(chunks):
    for chunk in chunks:
        chunk()


def halves(spot, load):
    return jnp.concatenate([flat(load(block)) for block in spot.pair()], axis=1)


def inside_kernel(weight, along_x, along_y, all_z, own, other, code, here, there, exponents, *fields):
    planes, rows = own.shape[2:4]
    steps = planes // 2
    spot = Spot(planes)
    sources = (own, other)

    def half(c, g, p):
        return halves(spot, lambda block: sources[g][:, c, p, :, block])

    def along_z():
        return jnp.concatenate([all_z[:, block] for block in spot.pair()], axis=1)

    def streamwise(field, p):
        return fill_x(field, along_y, along_z, lambda g: flat(sources[g][:, 1, p]), lambda g: half(2, g, p))

    def around(c, g, p):
        return jnp.concatenate([half(c, g, p + offset) for offset, _ in TAPS], axis=1)

    def summed(i, cell):
        return pair_sums(fields[i], weight, rows, there, here, cell)

    run(streamwise(fields[0], 0))

    @pl.loop(0, steps)
    def _(step):
        p = step + 2
        weave(summed(0, 2 * step), streamwise(fields[1], 2 * step + 1))
        weave(
            summed(1, 2 * step + 1),
            fill_z(fields[3], along_x, along_y, lambda g: half(0, g, p), lambda g: around(1, g, p)),
        )
        weave(
            summed(3, planes + steps + step),
            fill_y(
                fields[2], along_x, along_y, along_z,
                lambda g: flat(sources[g][:, 0, p]), lambda g: around(2, g, p),
            ),
        )
        weave(summed(2, planes + step), streamwise(fields[0], jnp.minimum(2 * step + 2, planes - 1)))

    encode(there, exponents, code, [(g * steps, g * steps + steps) for g in range(4)])


def edge_kernel(components, near, n_halos, halo_of, weight, along_x, along_y, all_z, own, other, *refs):
    count = len(components)
    halos, (code, here, there, exponents, *fields) = refs[:n_halos], refs[n_halos:]
    rows = own.shape[3]
    spot = Spot(own.shape[2])
    side = spot.near if near else spot.far
    sources = (own, other)

    def along_z():
        return jnp.concatenate([all_z[:, block] for block in spot.pair()], axis=1)

    def fill(n):
        c, p = components[n // 2], n % 2

        def around(g):
            return side.around(
                p,
                lambda i: halves(spot, lambda block: sources[g][:, c, side.own + i, :, block]),
                lambda i: flat(halo_of(halos, g)[:, c - components[0], i]),
            )

        if c == 2:
            return fill_y(
                fields[n % 2], along_x, along_y, along_z, lambda g: flat(sources[g][:, 0, side.edge + p]), around
            )
        return fill_z(
            fields[n % 2], along_x, along_y,
            lambda g: halves(spot, lambda block: sources[g][:, 0, side.edge + p, :, block]), around,
        )

    run(fill(0))
    for n in range(2 * count):
        weave(
            pair_sums(fields[n % 2], weight, rows, there, here, n),
            fill(n + 1) if n + 1 < 2 * count else [],
        )
    encode(there, exponents, code, [(2 * i, 2 * i + 2) for i in range(count)])


def solve(inverse, here, code, scales, cells, group, store):
    start, stop = cells
    count, groups = here.shape[0], scales.shape[0] // 3
    depth = here.shape[1]
    sums = []
    for j in range(count):
        coded = code[j * depth + start : j * depth + stop].astype(jnp.int32).astype(jnp.float32)
        sums.append(here[j, start:stop] + coded * scales[j * groups + group : j * groups + group + 1, :])
    for i in range(3):
        store(i, inverse[3 * i] * sums[0] + inverse[3 * i + 1] * sums[1] + inverse[3 * i + 2] * sums[2])


def finish_kernel(inverse, here, code, exponents, out, scales):
    planes = out.shape[3]
    half = planes // 2

    @pl.when(pl.program_id(0) == 0)
    def _():
        decode_scales(exponents[...], scales)

    rows = scales.shape[0] // ORDERS
    own = scales.at[pl.ds(pl.program_id(0) * rows, rows)]
    for group in range(4):
        cells = group * half, group * half + half

        def store(i, value, group=group):
            if group < 2:
                out[i, 0, 0, group * half : group * half + half] = value
            else:
                out[i, group - 1, 0, 2 : planes - 2] = value

        solve(inverse, here.at[0], code, own, cells, group, store)


def finish_edges_kernel(weight, inverse, along_x, along_y, own, other, across, diagonal, halo, *refs):
    near_here, near_code, far_here, far_code, _, out, near_out, far_out = refs[:8]
    near_scales, far_scales, *fields, out_sems = refs[8:]
    rows = own.shape[3]
    spot = Spot(own.shape[2])
    side, lane_here = spot.far, spot.lanes(spot.here)
    sources = (own, other, across, diagonal)

    def fill(p):
        def u(g):
            return flat(sources[g][:, 0, side.edge + p, :, lane_here] if g < 2 else sources[g][:, 4 + p])

        def own_plane(g, i):
            return flat(sources[g][:, 1, side.own + i, :, lane_here] if g < 2 else sources[g][:, i])

        def around(g):
            return side.around(p, lambda i: own_plane(g, i), lambda i: flat(halo[g, :, i]))

        return fill_z(fields[p], along_x, along_y, u, around)

    def solve_order(k):
        for c in range(2):
            def store_near(i, value, c=c):
                near_out[i, c, k] = value

            cells, scales = (2 - 2 * c, 4 - 2 * c), near_scales.at[pl.ds(6 * k, 6)]
            solve(inverse, near_here.at[k], near_code.at[pl.ds(12 * k, 12)], scales, cells, 1 - c, store_near)

        def store_far(i, value):
            far_out[i, 0, k] = value

        scales = far_scales.at[pl.ds(3 * k, 3)]
        solve(inverse, far_here.at[k], far_code.at[pl.ds(6 * k, 6)], scales, (0, 2), 0, store_far)

    def sum_half(p, half):
        def store(at, sums):
            for k in range(ORDERS):
                for i in range(3):
                    far_out[i, 1, k, p, at, :] = (
                        inverse[3 * i, at] * sums[0][k]
                        + inverse[3 * i + 1, at] * sums[1][k]
                        + inverse[3 * i + 2, at] * sums[2][k]
                    )

        power_sums(fields[p], weight, 0, half, rows, store)

    decode_scales(near_code[ORDERS * 12 :], near_scales)
    decode_scales(far_code[ORDERS * 6 :], far_scales)
    weave([lambda k=k: solve_order(k) for k in range(ORDERS)], fill(0))
    near_copy, far_copy = make_copies(
        [
            (near_out, out.at[:, pl.ds(1, 2), :, pl.ds(spot.near.edge, 2)]),
            (far_out, out.at[:, pl.ds(1, 2), :, pl.ds(spot.far.edge, 2)]),
        ],
        out_sems,
    )
    near_copy.start()
    weave([lambda half=half: sum_half(0, half) for half in range(rows // 8)], fill(1))
    for half in range(rows // 8):
        sum_half(1, half)
    far_copy.start()
    near_copy.wait()
    far_copy.wait()


def pack_near_kernel(own, near, sems):
    spot = Spot(own.shape[2])
    planes = pl.ds(spot.near.edge, 2)
    run_copies(
        [
            (own.at[:, pl.ds(1, 2), planes, :, block], near.at[:, :, :, :, pl.ds(b * 128, 128)])
            for b, block in enumerate(spot.pair())
        ],
        sems,
    )


def pack_across_kernel(own, across, diagonal, sems):
    spot = Spot(own.shape[2])
    pairs = []
    for target, block in ((across, spot.there), (diagonal, spot.diagonal)):
        lane = spot.lanes(block)
        pairs.append((own.at[:, 1, pl.ds(spot.far.own, 4), :, lane], target.at[:, pl.ds(0, 4)]))
        pairs.append((own.at[:, 0, pl.ds(spot.far.edge, 2), :, lane], target.at[:, pl.ds(4, 2)]))
    run_copies(pairs, sems)


def pack_other_kernel(own, other, near, far, sems):
    spot = Spot(own.shape[2])
    pairs = []
    for b, source in enumerate(spot.pair()):
        target = pl.ds(b * 128, 128)
        planes = pl.ds(spot.near.edge, 2)
        pairs.append((other.at[:, pl.ds(1, 2), planes, :, source], near.at[:, :, :, :, target]))
        planes = pl.ds(spot.far.edge, 2)
        for g, array in enumerate((own, other)):
            pairs.append((array.at[:, pl.ds(2, 1), planes, :, source], far.at[g, :, :, :, :, target]))
    run_copies(pairs, sems)


def pack_far_kernel(own, other, across, diagonal, far, sems):
    spot = Spot(own.shape[2])
    planes, lane = pl.ds(spot.far.edge, 2), spot.lanes(spot.here)
    pairs = [(array.at[:, 1, planes, :, lane], far.at[g]) for g, array in enumerate((own, other))]
    planes = pl.ds(spot.far.edge_at, 2)
    pairs += [(array.at[:, planes], far.at[2 + g]) for g, array in enumerate((across, diagonal))]
    run_copies(pairs, sems)


def params(megabytes):
    return {
        "compiler_params": pltpu.CompilerParams(vmem_limit_bytes=megabytes * 2**20),
        "cost_estimate": pl.CostEstimate(flops=1, bytes_accessed=1, transcendentals=0),
    }


def smem():
    return pl.BlockSpec(memory_space=pltpu.SMEM)


def hbm():
    return pl.BlockSpec(memory_space=pl.ANY)


def vmem():
    return pl.BlockSpec(memory_space=pltpu.VMEM)


def after(value, *others):
    return lax.optimization_barrier((value, *others))[0]


def local(velocity, phase_bins):
    snaps, _, planes, rows, lanes = velocity.shape
    kind = velocity.dtype
    n_snap, n_slab = lax.axis_size("snap"), lax.axis_size("slab")
    width = lanes // n_snap
    pair, size = 2 * width, snaps * rows

    near_pairs = [(i, i ^ 1) for i in range(n_slab)]
    far_pairs = [(i, i + 1) for i in range(1, n_slab - 1, 2)]
    far_pairs = far_pairs + [(j, i) for i, j in far_pairs]
    core_pairs = [(i, i ^ 1) for i in range(n_snap)]
    chip_pairs = [(i, (i + 2) % n_snap) for i in range(n_snap)]
    diagonal_pairs = [(i, ((i + 2) % n_snap) ^ 1) for i in range(n_snap)]

    def pack(kernel, arrays, shapes, copies):
        return pl.pallas_call(
            kernel,
            in_specs=[hbm()] * len(arrays),
            out_specs=[vmem()] * len(shapes),
            out_shape=[jax.ShapeDtypeStruct(shape, kind) for shape in shapes],
            scratch_shapes=[pltpu.SemaphoreType.DMA((copies,))],
            **params(8),
        )(*arrays)

    near_shape, far_shape = (snaps, 2, 2, rows, pair), (2, snaps, 1, 2, rows, pair)
    table = jnp.asarray(phase_table().reshape(-1))
    along_x = jnp.asarray(four_planes(pair), jnp.bfloat16)
    along_x_half = jnp.asarray(four_planes(width), jnp.bfloat16)
    along_y = jnp.asarray(np.kron(np.eye(snaps, dtype=np.float32), band(rows)), jnp.bfloat16)
    along_z = jnp.asarray(band(lanes).T, jnp.bfloat16)
    field = pltpu.VMEM((2 * size, pair), jnp.float32)

    def sums(cells, groups):
        shape = (ORDERS, 3, cells, rows, width)
        last = -(-ORDERS * 3 * groups // rows)
        return {
            "out_shape": [
                jax.ShapeDtypeStruct((ORDERS * 3 * cells + last, rows, width), jnp.int16),
                jax.ShapeDtypeStruct(shape, jnp.float32),
            ],
        }, [pltpu.VMEM(shape, jnp.float32), pltpu.VMEM((last * rows, width), jnp.float32)]

    def inside_sums(weights):
        call, scratch = sums(2 * planes, 4)
        return pl.pallas_call(
            inside_kernel, scratch_shapes=[*scratch, field, field, field, field], **call, **params(26)
        )(weights, along_x, along_y, along_z, velocity, other)

    def edge_sums(weights, components, near, halos, halo_of):
        count = len(components)

        def body(*refs):
            edge_kernel(components, near, len(halos), halo_of, *refs)

        call, scratch = sums(2 * count, count)
        return pl.pallas_call(body, scratch_shapes=[*scratch, field, field], **call, **params(26))(
            weights, along_x, along_y, along_z, velocity, other, *halos
        )

    def exchange(parts):
        code, here = parts
        return here, lax.ppermute(code, "snap", chip_pairs)

    other = lax.ppermute(velocity, "snap", core_pairs)
    with jax.named_scope("pack"):
        (near_own,) = pack(pack_near_kernel, (velocity,), [near_shape], 2)
        halo_own = lax.ppermute(near_own, "slab", near_pairs)
    pair_bins = jnp.concatenate([phase_bins, lax.ppermute(phase_bins, "snap", core_pairs)])
    chip_bins = [lax.ppermute(phase_bins, "snap", pairs) for pairs in (chip_pairs, diagonal_pairs)]
    all_bins = jnp.concatenate([pair_bins, *chip_bins])

    def spread(bins):
        return pl.pallas_call(
            weights_kernel,
            in_specs=[smem(), smem()],
            out_shape=jax.ShapeDtypeStruct((bins.shape[0], 2, 8, 128), jnp.float32),
            **params(8),
        )(bins, table)

    with jax.named_scope("weights"):
        pair_weights = spread(pair_bins)
    with jax.named_scope("pack"):
        for_across, for_diagonal = pack(
            pack_across_kernel, (after(velocity, near_own),), [(snaps, 6, rows, width)] * 2, 4
        )
        across = lax.ppermute(for_across, "snap", chip_pairs)
        diagonal = lax.ppermute(for_diagonal, "snap", diagonal_pairs)
        near_other, far_w = pack(
            pack_other_kernel, (velocity, after(other, for_across, for_diagonal)), [near_shape, far_shape], 6
        )
        halo_other = lax.ppermute(near_other, "slab", near_pairs)

    with jax.named_scope("inside"):
        inside_parts = inside_sums(after(pair_weights, near_other, far_w))

    with jax.named_scope("pack"):
        (far_v,) = pack(
            pack_far_kernel, (velocity, after(other, inside_parts[0], halo_own), across, diagonal), [(4, snaps, 2, rows, width)], 4
        )
    inside = exchange((after(inside_parts[0], far_v), inside_parts[1]))
    halo_w = lax.ppermute(after(far_w, inside_parts[0]), "slab", far_pairs)
    halo_v = lax.ppermute(after(far_v, halo_other), "slab", far_pairs)

    with jax.named_scope("edge_near"):
        near = exchange(edge_sums(pair_weights, (1, 2), True, (halo_own, halo_other), lambda halos, g: halos[g]))
    with jax.named_scope("edge_far"):
        ready = after(pair_weights, inside[1])
        far_y = exchange(edge_sums(ready, (2,), False, (halo_w,), lambda halos, g: halos[0].at[g]))

    with jax.named_scope("invert"):
        weights = spread(after(all_bins, inside_parts[0]))
        inverse = pl.pallas_call(
            invert_kernel, out_shape=jax.ShapeDtypeStruct((9, rows, width), jnp.float32), **params(8)
        )(weights)

    out_shape = jax.ShapeDtypeStruct((3, 3, ORDERS, planes, rows, width), jnp.float32)

    last = 3
    with jax.named_scope("finish"):
        out = pl.pallas_call(
            finish_kernel,
            out_shape=out_shape,
            grid=(ORDERS,),
            in_specs=[
                pl.BlockSpec((9, rows, width), lambda p: (0, 0, 0)),
                pl.BlockSpec((1, 3, 2 * planes, rows, width), lambda p: (p, 0, 0, 0, 0)),
                pl.BlockSpec((6 * planes, rows, width), lambda p: (p, 0, 0)),
                pl.BlockSpec((last, rows, width), lambda p: (ORDERS * 6 * planes // last, 0, 0)),
            ],
            out_specs=pl.BlockSpec((3, 3, 1, planes, rows, width), lambda p: (0, 0, p, 0, 0, 0)),
            scratch_shapes=[pltpu.VMEM((last * rows, width), jnp.float32)],
            **params(16),
        )(inverse, *inside, inside[1])

    with jax.named_scope("finish_edges"):
        edges = pltpu.VMEM((3, 2, ORDERS, 2, rows, width), jnp.float32)
        return pl.pallas_call(
            finish_edges_kernel,
            out_shape=out_shape,
            in_specs=[vmem()] * 13 + [hbm()],
            out_specs=hbm(),
            scratch_shapes=[
                edges, edges,
                pltpu.VMEM((2 * rows, width), jnp.float32),
                pltpu.VMEM((rows, width), jnp.float32),
                pltpu.VMEM((4 * size, width), jnp.float32),
                pltpu.VMEM((4 * size, width), jnp.float32),
                pltpu.SemaphoreType.DMA((2,)),
            ],
            input_output_aliases={13: 0},
            **params(26),
        )(
            weights, inverse, along_x_half, along_y, velocity, other, across, diagonal,
            after(halo_v, out), *near, *far_y, out,
        )


def solution(mesh):
    in_specs = (P("snap", None, "slab", None, None), P("snap"))
    out_specs = P(None, None, None, "slab", None, "snap")
    return jax.shard_map(local, mesh=mesh, in_specs=in_specs, out_specs=out_specs, check_vma=False)
```

```python
import jax
import jax.numpy as jnp
import numpy as np
from jax import lax
from jax.experimental import pallas as pl
from jax.experimental.pallas import tpu as pltpu
from jax.sharding import PartitionSpec as P

BINS = 180
ORDERS = 4
TAPS = ((-2, 1.0), (-1, -8.0), (1, 8.0), (2, -1.0))
STEP = 0.75 / 12.0
LEVELS = 32766.0
TINY = 1e-30


def band(size):
    matrix = np.zeros((size, size), np.float32)
    for offset, factor in TAPS:
        matrix += factor * np.eye(size, k=offset, dtype=np.float32)
    return matrix


def four_planes(width):
    return np.concatenate([factor * np.eye(width, dtype=np.float32) for _, factor in TAPS])


def phase_table():
    centers = (np.arange(BINS, dtype=np.float32) + np.float32(0.5)) * np.float32(2.0 * np.pi / BINS)
    return np.stack([np.cos(centers), np.sin(centers)], axis=1).astype(np.float32)


def weights_kernel(bins, table, weight, spread):
    for s in range(bins.shape[0]):
        weight[s, 0] = jnp.full(weight.shape[2:], table[bins[s] * 2], jnp.float32)
        weight[s, 1] = jnp.full(weight.shape[2:], table[bins[s] * 2 + 1], jnp.float32)
        spread[pl.ds(s, 1), :] = jnp.full((1, spread.shape[1]), bins[s], jnp.int32).astype(jnp.float32)


def invert_kernel(table, pair_weight, code, weight, inverse, received, bins, sem):
    count = pair_weight.shape[0]
    received[...] = code[code.shape[0] - count // code.shape[1] :].astype(jnp.int32).reshape(received.shape)
    copy = pltpu.make_async_copy(received, bins, sem)
    copy.start()
    weight[:count] = pair_weight[...]
    copy.wait()
    g01 = g02 = g11 = g12 = g22 = jnp.zeros(weight.shape[2:], jnp.float32)
    for s in range(weight.shape[0]):
        if s >= count:
            row = bins[s - count, 0] * 2
            weight[s, 0] = jnp.full(weight.shape[2:], table[row], jnp.float32)
            weight[s, 1] = jnp.full(weight.shape[2:], table[row + 1], jnp.float32)
        cosine, sine = weight[s, 0], weight[s, 1]
        g01, g02 = g01 + cosine, g02 + sine
        g11, g12, g22 = g11 + cosine * cosine, g12 + cosine * sine, g22 + sine * sine
    g00 = jnp.full(weight.shape[2:], weight.shape[0], jnp.float32)
    c00 = g11 * g22 - g12 * g12
    c01 = g02 * g12 - g01 * g22
    c02 = g01 * g12 - g02 * g11
    c11 = g00 * g22 - g02 * g02
    c12 = g02 * g01 - g00 * g12
    c22 = g00 * g11 - g01 * g01
    determinant = g00 * c00 + g01 * c01 + g02 * c02
    for i, entry in enumerate((c00, c01, c02, c01, c11, c12, c02, c12, c22)):
        for half in range(inverse.shape[1] // 8):
            inverse[i, pl.ds(half * 8, 8)] = entry / determinant


class Spot:
    def __init__(self, planes):
        snap, odd = lax.axis_index("snap"), lax.rem(lax.axis_index("slab"), 2)
        chip, core = lax.div(snap, 2), lax.rem(snap, 2)
        there, here = (1 - chip) * 2, chip * 2
        self.there, self.here, self.diagonal = there + core, here + core, there + 1 - core
        self.near, self.far = Side(planes, 1 - odd), Side(planes, odd)

    def lanes(self, block):
        return lanes_from(block * 128, 128)

    def pair(self):
        return self.lanes(self.there), self.lanes(self.here)


class Side:
    def __init__(self, planes, high):
        self.high = high == 1
        self.edge, self.own, self.own_at = high * (planes - 2), high * (planes - 4), 2 - high * 2
        self.halo_at, self.edge_at = high * 4, high * 2

    def around(self, p, own, halo):
        planes = []
        for offset, _ in TAPS:
            at = p + 2 + offset
            if at < 2:
                planes.append(jnp.where(self.high, own(at), halo(at)))
            elif at < 4:
                planes.append(own(at - self.own_at))
            else:
                planes.append(jnp.where(self.high, halo(at - 4), own(at - 2)))
        return jnp.concatenate(planes, axis=1)


def lanes_from(start, size):
    return pl.ds(pl.multiple_of(start, 128), size)


def power_sums(field, weight, lane, half, rows, store):
    total = [None] * (3 * ORDERS)
    for s in range(weight.shape[0]):
        first = field[pl.ds(s * rows + half * 8, 8), pl.ds(lane, 128)]
        second = first * first
        powers = (first, second, second * first, second * second)
        for j in range(3):
            for k in range(ORDERS):
                term = powers[k] if j == 0 else powers[k] * weight[s, j - 1]
                at = j * ORDERS + k
                total[at] = term if s == 0 else total[at] + term
    store(pl.ds(half * 8, 8), [[total[j * ORDERS + k] * STEP ** (k + 1) for k in range(ORDERS)] for j in range(3)])


def pair_sums(field, weight, rows, there, here, cell):
    def piece(half, lane, target):
        def store(at, sums):
            for j in range(3):
                for k in range(ORDERS):
                    target[k, j, cell, at, :] = sums[j][k]

        power_sums(field, weight, lane, half, rows, store)

    return [
        lambda half=half, lane=lane, target=target: piece(half, lane, target)
        for lane, target in ((0, there), (128, here))
        for half in range(rows // 8)
    ]


def weave(pieces, chunks):
    done = 0
    for i, piece in enumerate(pieces):
        piece()
        while done * len(pieces) < (i + 1) * len(chunks):
            chunks[done]()
            done += 1


def encode(sums, exponents, code, groups, bins=None):
    cells, rows = sums.shape[2:4]
    exponents[...] = jnp.zeros(exponents.shape, jnp.float32)
    for n in range(ORDERS * 3):
        for g, (start, stop) in enumerate(groups):
            value = sums[n // 3, n % 3, start:stop]
            top = jnp.max(jnp.max(jnp.abs(value), axis=0), axis=0, keepdims=True)
            exponent = jnp.ceil(jnp.log(jnp.maximum(top, TINY)) * np.float32(1.0 / np.log(2.0)))
            rounded = jnp.round(value * (jnp.exp2(-exponent) * LEVELS))
            code[n * cells + start : n * cells + stop] = rounded.astype(jnp.int32).astype(jnp.int16)
            exponents[pl.ds(n * len(groups) + g, 1), :] = exponent
    if bins is not None:
        exponents[exponents.shape[0] - bins.shape[0] :] = bins[...]
    last = exponents[...].reshape(exponents.shape[0] // rows, rows, exponents.shape[1])
    code[ORDERS * 3 * cells :] = last.astype(jnp.int32).astype(jnp.int16)


def decode_scales(code, scales):
    exponents = code.astype(jnp.int32).astype(jnp.float32)
    scales[...] = (jnp.exp2(exponents) * (1.0 / LEVELS)).reshape(scales.shape)


def flat(block):
    return block.reshape(block.shape[0] * block.shape[1], block.shape[2])


def product(a, b):
    return jnp.dot(a, b, preferred_element_type=jnp.float32)


def make_copies(pairs, sems):
    return [pltpu.make_async_copy(source, target, sems.at[i]) for i, (source, target) in enumerate(pairs)]


def run_copies(pairs, sems):
    copies = make_copies(pairs, sems)
    for copy in copies:
        copy.start()
    for copy in copies:
        copy.wait()


def fill_x(field, along_y, along_z, v, w):
    size = along_y.shape[0]

    def chunk(g):
        field[pl.ds(g * size, size), :] = product(along_y[...], w(g)) - product(v(g), along_z())

    return [lambda g=g: chunk(g) for g in range(field.shape[0] // size)]


def fill_y(field, along_x, along_y, along_z, u, planes):
    size = along_y.shape[0]

    def chunk(g):
        field[pl.ds(g * size, size), :] = product(u(g), along_z()) - product(planes(g), along_x[...])

    return [lambda g=g: chunk(g) for g in range(field.shape[0] // size)]


def fill_z(field, along_x, along_y, u, planes):
    size = along_y.shape[0]

    def chunk(g):
        field[pl.ds(g * size, size), :] = product(planes(g), along_x[...]) - product(along_y[...], u(g))

    return [lambda g=g: chunk(g) for g in range(field.shape[0] // size)]


def run(chunks):
    for chunk in chunks:
        chunk()


def halves(spot, load):
    return jnp.concatenate([flat(load(block)) for block in spot.pair()], axis=1)


def inside_kernel(bins, weight, along_x, along_y, all_z, own, other, code, here, there, exponents, *fields):
    planes, rows = own.shape[2:4]
    steps = planes // 2
    spot = Spot(planes)
    sources = (own, other)

    def half(c, g, p):
        return halves(spot, lambda block: sources[g][:, c, p, :, block])

    def along_z():
        return jnp.concatenate([all_z[:, block] for block in spot.pair()], axis=1)

    def streamwise(field, p):
        return fill_x(field, along_y, along_z, lambda g: flat(sources[g][:, 1, p]), lambda g: half(2, g, p))

    def around(c, g, p):
        return jnp.concatenate([half(c, g, p + offset) for offset, _ in TAPS], axis=1)

    def summed(i, cell):
        return pair_sums(fields[i], weight, rows, there, here, cell)

    run(streamwise(fields[0], 0))

    @pl.loop(0, steps)
    def _(step):
        p = step + 2
        weave(summed(0, 2 * step), streamwise(fields[1], 2 * step + 1))
        weave(
            summed(1, 2 * step + 1),
            fill_z(fields[3], along_x, along_y, lambda g: half(0, g, p), lambda g: around(1, g, p)),
        )
        weave(
            summed(3, planes + steps + step),
            fill_y(
                fields[2], along_x, along_y, along_z,
                lambda g: flat(sources[g][:, 0, p]), lambda g: around(2, g, p),
            ),
        )
        weave(summed(2, planes + step), streamwise(fields[0], jnp.minimum(2 * step + 2, planes - 1)))

    encode(there, exponents, code, [(g * steps, g * steps + steps) for g in range(4)], bins)


def edge_kernel(components, near, n_halos, halo_of, weight, along_x, along_y, all_z, own, other, *refs):
    count = len(components)
    halos, (code, here, there, exponents, *fields) = refs[:n_halos], refs[n_halos:]
    rows = own.shape[3]
    spot = Spot(own.shape[2])
    side = spot.near if near else spot.far
    sources = (own, other)

    def along_z():
        return jnp.concatenate([all_z[:, block] for block in spot.pair()], axis=1)

    def fill(n):
        c, p = components[n // 2], n % 2

        def around(g):
            return side.around(
                p,
                lambda i: halves(spot, lambda block: sources[g][:, c, side.own + i, :, block]),
                lambda i: flat(halo_of(halos, g)[:, c - components[0], i]),
            )

        if c == 2:
            return fill_y(
                fields[n % 2], along_x, along_y, along_z, lambda g: flat(sources[g][:, 0, side.edge + p]), around
            )
        return fill_z(
            fields[n % 2], along_x, along_y,
            lambda g: halves(spot, lambda block: sources[g][:, 0, side.edge + p, :, block]), around,
        )

    run(fill(0))
    for n in range(2 * count):
        weave(
            pair_sums(fields[n % 2], weight, rows, there, here, n),
            fill(n + 1) if n + 1 < 2 * count else [],
        )
    encode(there, exponents, code, [(2 * i, 2 * i + 2) for i in range(count)])


def solve(inverse, here, code, scales, cells, group, store):
    start, stop = cells
    count, groups = here.shape[0], scales.shape[0] // 3
    depth = here.shape[1]
    sums = []
    for j in range(count):
        coded = code[j * depth + start : j * depth + stop].astype(jnp.int32).astype(jnp.float32)
        sums.append(here[j, start:stop] + coded * scales[j * groups + group : j * groups + group + 1, :])
    for i in range(3):
        store(i, inverse[3 * i] * sums[0] + inverse[3 * i + 1] * sums[1] + inverse[3 * i + 2] * sums[2])


def finish_kernel(inverse, here, code, exponents, near_here, near_code, near_exponents, out, scales, near_scales):
    planes = out.shape[3]
    half = planes // 2
    edge = pl.ds(Spot(planes).near.edge, 2)

    @pl.when(pl.program_id(0) == 0)
    def _():
        decode_scales(exponents[...], scales)
        decode_scales(near_exponents[...], near_scales)

    inner = slice(2, planes - 2)
    targets = [(0, slice(0, half)), (0, slice(half, planes)), (1, inner), (2, inner), (2, edge), (1, edge)]
    for n, (component, at) in enumerate(targets):
        def store(i, value, component=component, at=at):
            out[i, component, 0, at] = value

        if n < 4:
            own = scales.at[pl.ds(pl.program_id(0) * 12, 12)]
            solve(inverse, here.at[0], code, own, (n * half, n * half + half), n, store)
        else:
            own = near_scales.at[pl.ds(pl.program_id(0) * 6, 6)]
            solve(inverse, near_here.at[0], near_code, own, (2 * n - 8, 2 * n - 6), n - 4, store)


def finish_far_kernel(weight, inverse, along_x, along_y, own, other, across, diagonal, halo, *refs):
    far_here, far_code, _, out, far_out, far_scales, *fields, out_sem = refs
    rows = own.shape[3]
    spot = Spot(own.shape[2])
    side, lane_here = spot.far, spot.lanes(spot.here)
    sources = (own, other, across, diagonal)

    def fill(p):
        def u(g):
            return flat(sources[g][:, 0, side.edge + p, :, lane_here] if g < 2 else sources[g][:, 4 + p])

        def own_plane(g, i):
            return flat(sources[g][:, 1, side.own + i, :, lane_here] if g < 2 else sources[g][:, i])

        def around(g):
            return side.around(p, lambda i: own_plane(g, i), lambda i: flat(halo[g, :, i]))

        return fill_z(fields[p], along_x, along_y, u, around)

    def solve_order(k):
        def store_far(i, value):
            far_out[i, 0, k] = value

        scales = far_scales.at[pl.ds(3 * k, 3)]
        solve(inverse, far_here.at[k], far_code.at[pl.ds(6 * k, 6)], scales, (0, 2), 0, store_far)

    def sum_half(p, half):
        def store(at, sums):
            for k in range(ORDERS):
                for i in range(3):
                    far_out[i, 1, k, p, at, :] = (
                        inverse[3 * i, at] * sums[0][k]
                        + inverse[3 * i + 1, at] * sums[1][k]
                        + inverse[3 * i + 2, at] * sums[2][k]
                    )

        power_sums(fields[p], weight, 0, half, rows, store)

    decode_scales(far_code[ORDERS * 6 :], far_scales)
    weave([lambda k=k: solve_order(k) for k in range(ORDERS)], fill(0))
    weave([lambda half=half: sum_half(0, half) for half in range(rows // 8)], fill(1))
    for half in range(rows // 8):
        sum_half(1, half)
    copy = pltpu.make_async_copy(far_out, out.at[:, pl.ds(1, 2), :, pl.ds(side.edge, 2)], out_sem)
    copy.start()
    copy.wait()


def pack_near_kernel(own, near, sems):
    spot = Spot(own.shape[2])
    planes = pl.ds(spot.near.edge, 2)
    run_copies(
        [
            (own.at[:, pl.ds(1, 2), planes, :, block], near.at[:, :, :, :, pl.ds(b * 128, 128)])
            for b, block in enumerate(spot.pair())
        ],
        sems,
    )


def pack_across_kernel(own, across, diagonal, sems):
    spot = Spot(own.shape[2])
    pairs = []
    for target, block in ((across, spot.there), (diagonal, spot.diagonal)):
        lane = spot.lanes(block)
        pairs.append((own.at[:, 1, pl.ds(spot.far.own, 4), :, lane], target.at[:, pl.ds(0, 4)]))
        pairs.append((own.at[:, 0, pl.ds(spot.far.edge, 2), :, lane], target.at[:, pl.ds(4, 2)]))
    run_copies(pairs, sems)


def pack_other_kernel(own, other, near, far, sems):
    spot = Spot(own.shape[2])
    pairs = []
    for b, source in enumerate(spot.pair()):
        target = pl.ds(b * 128, 128)
        planes = pl.ds(spot.near.edge, 2)
        pairs.append((other.at[:, pl.ds(1, 2), planes, :, source], near.at[:, :, :, :, target]))
        planes = pl.ds(spot.far.edge, 2)
        for g, array in enumerate((own, other)):
            pairs.append((array.at[:, pl.ds(2, 1), planes, :, source], far.at[g, :, :, :, :, target]))
    run_copies(pairs, sems)


def pack_far_kernel(own, other, across, diagonal, far, sems):
    spot = Spot(own.shape[2])
    planes, lane = pl.ds(spot.far.edge, 2), spot.lanes(spot.here)
    pairs = [(array.at[:, 1, planes, :, lane], far.at[g]) for g, array in enumerate((own, other))]
    planes = pl.ds(spot.far.edge_at, 2)
    pairs += [(array.at[:, planes], far.at[2 + g]) for g, array in enumerate((across, diagonal))]
    run_copies(pairs, sems)


def params(megabytes):
    return {
        "compiler_params": pltpu.CompilerParams(vmem_limit_bytes=megabytes * 2**20),
        "cost_estimate": pl.CostEstimate(flops=1, bytes_accessed=1, transcendentals=0),
    }


def smem():
    return pl.BlockSpec(memory_space=pltpu.SMEM)


def hbm():
    return pl.BlockSpec(memory_space=pl.ANY)


def vmem():
    return pl.BlockSpec(memory_space=pltpu.VMEM)


def after(value, *others):
    return lax.optimization_barrier((value, *others))[0]


def local(velocity, phase_bins):
    snaps, _, planes, rows, lanes = velocity.shape
    kind = velocity.dtype
    n_snap, n_slab = lax.axis_size("snap"), lax.axis_size("slab")
    width = lanes // n_snap
    pair, size = 2 * width, snaps * rows

    near_pairs = [(i, i ^ 1) for i in range(n_slab)]
    far_pairs = [(i, i + 1) for i in range(1, n_slab - 1, 2)]
    far_pairs = far_pairs + [(j, i) for i, j in far_pairs]
    core_pairs = [(i, i ^ 1) for i in range(n_snap)]
    chip_pairs = [(i, (i + 2) % n_snap) for i in range(n_snap)]
    diagonal_pairs = [(i, ((i + 2) % n_snap) ^ 1) for i in range(n_snap)]

    def pack(kernel, arrays, shapes, copies, megabytes=8):
        return pl.pallas_call(
            kernel,
            in_specs=[hbm()] * len(arrays),
            out_specs=[vmem()] * len(shapes),
            out_shape=[jax.ShapeDtypeStruct(shape, kind) for shape in shapes],
            scratch_shapes=[pltpu.SemaphoreType.DMA((copies,))],
            **params(megabytes),
        )(*arrays)

    near_shape, far_shape = (snaps, 2, 2, rows, pair), (2, snaps, 1, 2, rows, pair)
    table = jnp.asarray(phase_table().reshape(-1))
    along_x = jnp.asarray(four_planes(pair), jnp.bfloat16)
    along_x_half = jnp.asarray(four_planes(width), jnp.bfloat16)
    along_y = jnp.asarray(np.kron(np.eye(snaps, dtype=np.float32), band(rows)), jnp.bfloat16)
    along_z = jnp.asarray(band(lanes).T, jnp.bfloat16)
    field = pltpu.VMEM((2 * size, pair), jnp.float32)

    def sums(cells, groups, extra=0):
        shape = (ORDERS, 3, cells, rows, width)
        last = -(-(ORDERS * 3 * groups + extra) // rows)
        return {
            "out_shape": [
                jax.ShapeDtypeStruct((ORDERS * 3 * cells + last, rows, width), jnp.int16),
                jax.ShapeDtypeStruct(shape, jnp.float32),
            ],
        }, [pltpu.VMEM(shape, jnp.float32), pltpu.VMEM((last * rows, width), jnp.float32)]

    def inside_sums(weights):
        call, scratch = sums(2 * planes, 4, 2 * snaps)
        return pl.pallas_call(
            inside_kernel,
            scratch_shapes=[*scratch, field, field, field, field],
            **call, **params(26),
        )(spread_bins, weights, along_x, along_y, along_z, velocity, other)

    def edge_sums(weights, components, near, halos, halo_of):
        count = len(components)

        def body(*refs):
            edge_kernel(components, near, len(halos), halo_of, *refs)

        call, scratch = sums(2 * count, count)
        return pl.pallas_call(body, scratch_shapes=[*scratch, field, field], **call, **params(26))(
            weights, along_x, along_y, along_z, velocity, other, *halos
        )

    def exchange(parts):
        code, here = parts
        return here, lax.ppermute(code, "snap", chip_pairs)

    other = lax.ppermute(velocity, "snap", core_pairs)
    with jax.named_scope("pack"):
        (near_own,) = pack(pack_near_kernel, (velocity,), [near_shape], 2, 51)
        halo_own = lax.ppermute(near_own, "slab", near_pairs)
    pair_bins = jnp.concatenate([phase_bins, lax.ppermute(phase_bins, "snap", core_pairs)])

    with jax.named_scope("weights"):
        pair_weights, spread_bins = pl.pallas_call(
            weights_kernel,
            in_specs=[smem(), smem()],
            out_shape=[
                jax.ShapeDtypeStruct((2 * snaps, 2, 8, 128), jnp.float32),
                jax.ShapeDtypeStruct((2 * snaps, width), jnp.float32),
            ],
            **params(8),
        )(pair_bins, table)
    with jax.named_scope("pack"):
        for_across, for_diagonal = pack(
            pack_across_kernel, (after(velocity, near_own),), [(snaps, 6, rows, width)] * 2, 4
        )
        across = lax.ppermute(for_across, "snap", chip_pairs)
        diagonal = lax.ppermute(for_diagonal, "snap", diagonal_pairs)
        near_other, far_w = pack(
            pack_other_kernel, (velocity, after(other, for_across, for_diagonal)), [near_shape, far_shape], 6
        )
        halo_other = lax.ppermute(near_other, "slab", near_pairs)

    with jax.named_scope("inside"):
        inside_parts = inside_sums(after(pair_weights, near_other, far_w))

    with jax.named_scope("pack"):
        (far_v,) = pack(
            pack_far_kernel, (velocity, after(other, inside_parts[0], halo_own), across, diagonal), [(4, snaps, 2, rows, width)], 4
        )
    inside = exchange((after(inside_parts[0], far_v), inside_parts[1]))
    halo_w = lax.ppermute(after(far_w, inside_parts[0]), "slab", far_pairs)
    halo_v = lax.ppermute(after(far_v, halo_other), "slab", far_pairs)

    with jax.named_scope("edge_near"):
        near = exchange(edge_sums(pair_weights, (1, 2), True, (halo_own, halo_other), lambda halos, g: halos[g]))
    with jax.named_scope("edge_far"):
        ready = pair_weights
        far_y = exchange(edge_sums(ready, (2,), False, (halo_w,), lambda halos, g: halos[0].at[g]))

    with jax.named_scope("invert"):
        weights, inverse = pl.pallas_call(
            invert_kernel,
            in_specs=[smem(), vmem(), vmem()],
            out_shape=[
                jax.ShapeDtypeStruct((4 * snaps, 2, 8, 128), jnp.float32),
                jax.ShapeDtypeStruct((9, rows, width), jnp.float32),
            ],
            scratch_shapes=[
                pltpu.VMEM((2 * snaps, width), jnp.int32),
                pltpu.SMEM((2 * snaps, width), jnp.int32),
                pltpu.SemaphoreType.DMA,
            ],
            **params(8),
        )(table, pair_weights, inside[1])

    out_shape = jax.ShapeDtypeStruct((3, 3, ORDERS, planes, rows, width), jnp.float32)

    lasts = 3, 2

    def one_order(parts, last):
        cells = parts[0].shape[2]
        return [
            pl.BlockSpec((1, 3, cells, rows, width), lambda p: (p, 0, 0, 0, 0)),
            pl.BlockSpec((3 * cells, rows, width), lambda p: (p, 0, 0)),
            pl.BlockSpec((last, rows, width), lambda p: (ORDERS * 3 * cells // last, 0, 0)),
        ]

    with jax.named_scope("finish"):
        out = pl.pallas_call(
            finish_kernel,
            out_shape=out_shape,
            grid=(ORDERS,),
            in_specs=[
                pl.BlockSpec((9, rows, width), lambda p: (0, 0, 0)),
                *one_order(inside, lasts[0]), *one_order(near, lasts[1]),
            ],
            out_specs=pl.BlockSpec((3, 3, 1, planes, rows, width), lambda p: (0, 0, p, 0, 0, 0)),
            scratch_shapes=[pltpu.VMEM((last * rows, width), jnp.float32) for last in lasts],
            **params(16),
        )(inverse, *inside, inside[1], *near, near[1])

    with jax.named_scope("finish_far"):
        edges = pltpu.VMEM((3, 2, ORDERS, 2, rows, width), jnp.float32)
        return pl.pallas_call(
            finish_far_kernel,
            out_shape=out_shape,
            in_specs=[vmem()] * 11 + [hbm()],
            out_specs=hbm(),
            scratch_shapes=[
                edges,
                pltpu.VMEM((rows, width), jnp.float32),
                pltpu.VMEM((4 * size, width), jnp.float32),
                pltpu.VMEM((4 * size, width), jnp.float32),
                pltpu.SemaphoreType.DMA,
            ],
            input_output_aliases={11: 0},
            **params(26),
        )(
            weights, inverse, along_x_half, along_y, velocity, other, across, diagonal,
            after(halo_v, out), *far_y, out,
        )


def solution(mesh):
    in_specs = (P("snap", None, "slab", None, None), P("snap"))
    out_specs = P(None, None, None, "slab", None, "snap")
    return jax.shard_map(local, mesh=mesh, in_specs=in_specs, out_specs=out_specs, check_vma=False)
```

```python
import jax
import jax.numpy as jnp
import numpy as np
from jax import lax
from jax.experimental import pallas as pl
from jax.experimental.pallas import tpu as pltpu
from jax.sharding import PartitionSpec as P

BINS = 180
ORDERS = 4
TAPS = ((-2, 1.0), (-1, -8.0), (1, 8.0), (2, -1.0))
STEP = 0.75 / 12.0
LEVELS = 32766.0
TINY = 1e-30


def band(size):
    matrix = np.zeros((size, size), np.float32)
    for offset, factor in TAPS:
        matrix += factor * np.eye(size, k=offset, dtype=np.float32)
    return matrix


def four_planes(width):
    return np.concatenate([factor * np.eye(width, dtype=np.float32) for _, factor in TAPS])


def phase_table():
    centers = (np.arange(BINS, dtype=np.float32) + np.float32(0.5)) * np.float32(2.0 * np.pi / BINS)
    return np.stack([np.cos(centers), np.sin(centers)], axis=1).astype(np.float32)


def weights_kernel(bins, table, weight, spread):
    for s in range(bins.shape[0]):
        weight[s, 0] = jnp.full(weight.shape[2:], table[bins[s] * 2], jnp.float32)
        weight[s, 1] = jnp.full(weight.shape[2:], table[bins[s] * 2 + 1], jnp.float32)
        spread[pl.ds(s, 1), :] = jnp.full((1, spread.shape[1]), bins[s], jnp.int32).astype(jnp.float32)


def invert_kernel(table, pair_weight, code, weight, inverse, received, bins, sem):
    count = pair_weight.shape[0]
    received[...] = code[code.shape[0] - count // code.shape[1] :].astype(jnp.int32).reshape(received.shape)
    copy = pltpu.make_async_copy(received, bins, sem)
    copy.start()
    weight[:count] = pair_weight[...]
    copy.wait()
    g01 = g02 = g11 = g12 = g22 = jnp.zeros(weight.shape[2:], jnp.float32)
    for s in range(weight.shape[0]):
        if s >= count:
            row = bins[s - count, 0] * 2
            weight[s, 0] = jnp.full(weight.shape[2:], table[row], jnp.float32)
            weight[s, 1] = jnp.full(weight.shape[2:], table[row + 1], jnp.float32)
        cosine, sine = weight[s, 0], weight[s, 1]
        g01, g02 = g01 + cosine, g02 + sine
        g11, g12, g22 = g11 + cosine * cosine, g12 + cosine * sine, g22 + sine * sine
    g00 = jnp.full(weight.shape[2:], weight.shape[0], jnp.float32)
    c00 = g11 * g22 - g12 * g12
    c01 = g02 * g12 - g01 * g22
    c02 = g01 * g12 - g02 * g11
    c11 = g00 * g22 - g02 * g02
    c12 = g02 * g01 - g00 * g12
    c22 = g00 * g11 - g01 * g01
    determinant = g00 * c00 + g01 * c01 + g02 * c02
    for i, entry in enumerate((c00, c01, c02, c01, c11, c12, c02, c12, c22)):
        for half in range(inverse.shape[1] // 8):
            inverse[i, pl.ds(half * 8, 8)] = entry / determinant


class Spot:
    def __init__(self, planes):
        snap, odd = lax.axis_index("snap"), lax.rem(lax.axis_index("slab"), 2)
        chip, core = lax.div(snap, 2), lax.rem(snap, 2)
        there, here = (1 - chip) * 2, chip * 2
        self.there, self.here, self.diagonal = there + core, here + core, there + 1 - core
        self.near, self.far = Side(planes, 1 - odd), Side(planes, odd)

    def lanes(self, block):
        return lanes_from(block * 128, 128)

    def pair(self):
        return self.lanes(self.there), self.lanes(self.here)


class Side:
    def __init__(self, planes, high):
        self.high = high == 1
        self.edge, self.own, self.own_at = high * (planes - 2), high * (planes - 4), 2 - high * 2
        self.halo_at, self.edge_at = high * 4, high * 2

    def around(self, p, own, halo):
        planes = []
        for offset, _ in TAPS:
            at = p + 2 + offset
            if at < 2:
                planes.append(jnp.where(self.high, own(at), halo(at)))
            elif at < 4:
                planes.append(own(at - self.own_at))
            else:
                planes.append(jnp.where(self.high, halo(at - 4), own(at - 2)))
        return jnp.concatenate(planes, axis=1)


def lanes_from(start, size):
    return pl.ds(pl.multiple_of(start, 128), size)


def power_sums(field, weight, lane, half, rows, store):
    total = [None] * (3 * ORDERS)
    for s in range(weight.shape[0]):
        first = field[pl.ds(s * rows + half * 8, 8), pl.ds(lane, 128)]
        second = first * first
        powers = (first, second, second * first, second * second)
        for j in range(3):
            for k in range(ORDERS):
                term = powers[k] if j == 0 else powers[k] * weight[s, j - 1]
                at = j * ORDERS + k
                total[at] = term if s == 0 else total[at] + term
    store(pl.ds(half * 8, 8), [[total[j * ORDERS + k] * STEP ** (k + 1) for k in range(ORDERS)] for j in range(3)])


def pair_sums(field, weight, rows, there, here, cell):
    def piece(half, lane, target):
        def store(at, sums):
            for j in range(3):
                for k in range(ORDERS):
                    target[k, j, cell, at, :] = sums[j][k]

        power_sums(field, weight, lane, half, rows, store)

    return [
        lambda half=half, lane=lane, target=target: piece(half, lane, target)
        for lane, target in ((0, there), (128, here))
        for half in range(rows // 8)
    ]


def weave(pieces, chunks):
    done = 0
    for i, piece in enumerate(pieces):
        piece()
        while done * len(pieces) < (i + 1) * len(chunks):
            chunks[done]()
            done += 1


def encode(sums, exponents, code, groups, bins=None):
    cells, rows = sums.shape[2:4]
    exponents[...] = jnp.zeros(exponents.shape, jnp.float32)
    for n in range(ORDERS * 3):
        for g, (start, stop) in enumerate(groups):
            value = sums[n // 3, n % 3, start:stop]
            top = jnp.max(jnp.max(jnp.abs(value), axis=0), axis=0, keepdims=True)
            exponent = jnp.ceil(jnp.log(jnp.maximum(top, TINY)) * np.float32(1.0 / np.log(2.0)))
            rounded = jnp.round(value * (jnp.exp2(-exponent) * LEVELS))
            code[n * cells + start : n * cells + stop] = rounded.astype(jnp.int32).astype(jnp.int16)
            exponents[pl.ds(n * len(groups) + g, 1), :] = exponent
    if bins is not None:
        exponents[exponents.shape[0] - bins.shape[0] :] = bins[...]
    last = exponents[...].reshape(exponents.shape[0] // rows, rows, exponents.shape[1])
    code[ORDERS * 3 * cells :] = last.astype(jnp.int32).astype(jnp.int16)


def decode_scales(code, scales):
    exponents = code.astype(jnp.int32).astype(jnp.float32)
    scales[...] = (jnp.exp2(exponents) * (1.0 / LEVELS)).reshape(scales.shape)


def flat(block):
    return block.reshape(block.shape[0] * block.shape[1], block.shape[2])


def product(a, b):
    return jnp.dot(a, b, preferred_element_type=jnp.float32)


def make_copies(pairs, sems):
    return [pltpu.make_async_copy(source, target, sems.at[i]) for i, (source, target) in enumerate(pairs)]


def run_copies(pairs, sems):
    copies = make_copies(pairs, sems)
    for copy in copies:
        copy.start()
    for copy in copies:
        copy.wait()


def fill_x(field, along_y, along_z, v, w):
    size = along_y.shape[0]

    def chunk(g):
        field[pl.ds(g * size, size), :] = product(along_y[...], w(g)) - product(v(g), along_z())

    return [lambda g=g: chunk(g) for g in range(field.shape[0] // size)]


def fill_y(field, along_x, along_y, along_z, u, planes):
    size = along_y.shape[0]

    def chunk(g):
        field[pl.ds(g * size, size), :] = product(u(g), along_z()) - product(planes(g), along_x[...])

    return [lambda g=g: chunk(g) for g in range(field.shape[0] // size)]


def fill_z(field, along_x, along_y, u, planes):
    size = along_y.shape[0]

    def chunk(g):
        field[pl.ds(g * size, size), :] = product(planes(g), along_x[...]) - product(along_y[...], u(g))

    return [lambda g=g: chunk(g) for g in range(field.shape[0] // size)]


def run(chunks):
    for chunk in chunks:
        chunk()


def halves(spot, load):
    return jnp.concatenate([flat(load(block)) for block in spot.pair()], axis=1)


def inside_kernel(bins, weight, along_x, along_y, all_z, own, other, code, here, there, exponents, *fields):
    planes, rows = own.shape[2:4]
    steps = planes // 2
    spot = Spot(planes)
    sources = (own, other)

    def half(c, g, p):
        return halves(spot, lambda block: sources[g][:, c, p, :, block])

    def along_z():
        return jnp.concatenate([all_z[:, block] for block in spot.pair()], axis=1)

    def streamwise(field, p):
        return fill_x(field, along_y, along_z, lambda g: flat(sources[g][:, 1, p]), lambda g: half(2, g, p))

    def around(c, g, p):
        return jnp.concatenate([half(c, g, p + offset) for offset, _ in TAPS], axis=1)

    def summed(i, cell):
        return pair_sums(fields[i], weight, rows, there, here, cell)

    run(streamwise(fields[0], 0))

    @pl.loop(0, steps)
    def _(step):
        p = step + 2
        weave(summed(0, 2 * step), streamwise(fields[1], 2 * step + 1))
        weave(
            summed(1, 2 * step + 1),
            fill_z(fields[3], along_x, along_y, lambda g: half(0, g, p), lambda g: around(1, g, p)),
        )
        weave(
            summed(3, planes + steps + step),
            fill_y(
                fields[2], along_x, along_y, along_z,
                lambda g: flat(sources[g][:, 0, p]), lambda g: around(2, g, p),
            ),
        )
        weave(summed(2, planes + step), streamwise(fields[0], jnp.minimum(2 * step + 2, planes - 1)))

    encode(there, exponents, code, [(g * steps, g * steps + steps) for g in range(4)], bins)


def edge_kernel(components, near, n_halos, halo_of, weight, along_x, along_y, all_z, own, other, *refs):
    count = len(components)
    halos, (code, here, there, exponents, *fields) = refs[:n_halos], refs[n_halos:]
    rows = own.shape[3]
    spot = Spot(own.shape[2])
    side = spot.near if near else spot.far
    sources = (own, other)

    def along_z():
        return jnp.concatenate([all_z[:, block] for block in spot.pair()], axis=1)

    def fill(n):
        c, p = components[n // 2], n % 2

        def around(g):
            return side.around(
                p,
                lambda i: halves(spot, lambda block: sources[g][:, c, side.own + i, :, block]),
                lambda i: flat(halo_of(halos, g)[:, c - components[0], i]),
            )

        if c == 2:
            return fill_y(
                fields[n % 2], along_x, along_y, along_z, lambda g: flat(sources[g][:, 0, side.edge + p]), around
            )
        return fill_z(
            fields[n % 2], along_x, along_y,
            lambda g: halves(spot, lambda block: sources[g][:, 0, side.edge + p, :, block]), around,
        )

    run(fill(0))
    for n in range(2 * count):
        weave(
            pair_sums(fields[n % 2], weight, rows, there, here, n),
            fill(n + 1) if n + 1 < 2 * count else [],
        )
    encode(there, exponents, code, [(2 * i, 2 * i + 2) for i in range(count)])


def solve(inverse, here, code, scales, cells, group, store):
    start, stop = cells
    count, groups = here.shape[0], scales.shape[0] // 3
    depth = here.shape[1]
    sums = []
    for j in range(count):
        coded = code[j * depth + start : j * depth + stop].astype(jnp.int32).astype(jnp.float32)
        sums.append(here[j, start:stop] + coded * scales[j * groups + group : j * groups + group + 1, :])
    for i in range(3):
        store(i, inverse[3 * i] * sums[0] + inverse[3 * i + 1] * sums[1] + inverse[3 * i + 2] * sums[2])


def finish_kernel(inverse, here, code, exponents, near_here, near_code, near_exponents, out, scales, near_scales):
    planes = out.shape[3]
    half = planes // 2
    edge = pl.ds(Spot(planes).near.edge, 2)

    @pl.when(pl.program_id(0) == 0)
    def _():
        decode_scales(exponents[...], scales)
        decode_scales(near_exponents[...], near_scales)

    inner = slice(2, planes - 2)
    targets = [(0, slice(0, half)), (0, slice(half, planes)), (1, inner), (2, inner), (2, edge), (1, edge)]
    for n, (component, at) in enumerate(targets):
        def store(i, value, component=component, at=at):
            out[i, component, 0, at] = value

        if n < 4:
            own = scales.at[pl.ds(pl.program_id(0) * 12, 12)]
            solve(inverse, here.at[0], code, own, (n * half, n * half + half), n, store)
        else:
            own = near_scales.at[pl.ds(pl.program_id(0) * 6, 6)]
            solve(inverse, near_here.at[0], near_code, own, (2 * n - 8, 2 * n - 6), n - 4, store)


def finish_far_kernel(weight, inverse, along_x, along_y, own, other, across, diagonal, halo, *refs):
    far_here, far_code, _, out, far_out, far_scales, *fields, out_sem = refs
    rows = own.shape[3]
    spot = Spot(own.shape[2])
    side, lane_here = spot.far, spot.lanes(spot.here)
    sources = (own, other, across, diagonal)

    def fill(p):
        def u(g):
            return flat(sources[g][:, 0, side.edge + p, :, lane_here] if g < 2 else sources[g][:, 4 + p])

        def own_plane(g, i):
            return flat(sources[g][:, 1, side.own + i, :, lane_here] if g < 2 else sources[g][:, i])

        def around(g):
            return side.around(p, lambda i: own_plane(g, i), lambda i: flat(halo[g, :, i]))

        return fill_z(fields[p], along_x, along_y, u, around)

    def solve_order(k):
        def store_far(i, value):
            far_out[i, 0, k] = value

        scales = far_scales.at[pl.ds(3 * k, 3)]
        solve(inverse, far_here.at[k], far_code.at[pl.ds(6 * k, 6)], scales, (0, 2), 0, store_far)

    def sum_half(p, half):
        def store(at, sums):
            for k in range(ORDERS):
                for i in range(3):
                    far_out[i, 1, k, p, at, :] = (
                        inverse[3 * i, at] * sums[0][k]
                        + inverse[3 * i + 1, at] * sums[1][k]
                        + inverse[3 * i + 2, at] * sums[2][k]
                    )

        power_sums(fields[p], weight, 0, half, rows, store)

    decode_scales(far_code[ORDERS * 6 :], far_scales)
    weave([lambda k=k: solve_order(k) for k in range(ORDERS)], fill(0))
    weave([lambda half=half: sum_half(0, half) for half in range(rows // 8)], fill(1))
    for half in range(rows // 8):
        sum_half(1, half)
    copy = pltpu.make_async_copy(far_out, out.at[:, pl.ds(1, 2), :, pl.ds(side.edge, 2)], out_sem)
    copy.start()
    copy.wait()


def pack_near_kernel(own, near, sems):
    spot = Spot(own.shape[2])
    planes = pl.ds(spot.near.edge, 2)
    run_copies(
        [
            (own.at[:, pl.ds(1, 2), planes, :, block], near.at[:, :, :, :, pl.ds(b * 128, 128)])
            for b, block in enumerate(spot.pair())
        ],
        sems,
    )


def pack_across_kernel(own, across, diagonal, sems):
    spot = Spot(own.shape[2])
    pairs = []
    for target, block in ((across, spot.there), (diagonal, spot.diagonal)):
        lane = spot.lanes(block)
        pairs.append((own.at[:, 1, pl.ds(spot.far.own, 4), :, lane], target.at[:, pl.ds(0, 4)]))
        pairs.append((own.at[:, 0, pl.ds(spot.far.edge, 2), :, lane], target.at[:, pl.ds(4, 2)]))
    run_copies(pairs, sems)


def pack_other_kernel(own, other, near, far, sems):
    spot = Spot(own.shape[2])
    pairs = []
    for b, source in enumerate(spot.pair()):
        target = pl.ds(b * 128, 128)
        planes = pl.ds(spot.near.edge, 2)
        pairs.append((other.at[:, pl.ds(1, 2), planes, :, source], near.at[:, :, :, :, target]))
        planes = pl.ds(spot.far.edge, 2)
        for g, array in enumerate((own, other)):
            pairs.append((array.at[:, pl.ds(2, 1), planes, :, source], far.at[g, :, :, :, :, target]))
    run_copies(pairs, sems)


def pack_far_kernel(own, other, across, diagonal, far, sems):
    spot = Spot(own.shape[2])
    planes, lane = pl.ds(spot.far.edge, 2), spot.lanes(spot.here)
    pairs = [(array.at[:, 1, planes, :, lane], far.at[g]) for g, array in enumerate((own, other))]
    planes = pl.ds(spot.far.edge_at, 2)
    pairs += [(array.at[:, planes], far.at[2 + g]) for g, array in enumerate((across, diagonal))]
    run_copies(pairs, sems)


def params(megabytes):
    return {
        "compiler_params": pltpu.CompilerParams(vmem_limit_bytes=megabytes * 2**20),
        "cost_estimate": pl.CostEstimate(flops=1, bytes_accessed=1, transcendentals=0),
    }


def smem():
    return pl.BlockSpec(memory_space=pltpu.SMEM)


def hbm():
    return pl.BlockSpec(memory_space=pl.ANY)


def vmem():
    return pl.BlockSpec(memory_space=pltpu.VMEM)


def after(value, *others):
    return lax.optimization_barrier((value, *others))[0]


def local(velocity, phase_bins):
    snaps, _, planes, rows, lanes = velocity.shape
    kind = velocity.dtype
    n_snap, n_slab = lax.axis_size("snap"), lax.axis_size("slab")
    width = lanes // n_snap
    pair, size = 2 * width, snaps * rows

    near_pairs = [(i, i ^ 1) for i in range(n_slab)]
    far_pairs = [(i, i + 1) for i in range(1, n_slab - 1, 2)]
    far_pairs = far_pairs + [(j, i) for i, j in far_pairs]
    core_pairs = [(i, i ^ 1) for i in range(n_snap)]
    chip_pairs = [(i, (i + 2) % n_snap) for i in range(n_snap)]
    diagonal_pairs = [(i, ((i + 2) % n_snap) ^ 1) for i in range(n_snap)]

    def pack(kernel, arrays, shapes, copies, megabytes=8):
        return pl.pallas_call(
            kernel,
            in_specs=[hbm()] * len(arrays),
            out_specs=[vmem()] * len(shapes),
            out_shape=[jax.ShapeDtypeStruct(shape, kind) for shape in shapes],
            scratch_shapes=[pltpu.SemaphoreType.DMA((copies,))],
            **params(megabytes),
        )(*arrays)

    near_shape, far_shape = (snaps, 2, 2, rows, pair), (2, snaps, 1, 2, rows, pair)
    table = jnp.asarray(phase_table().reshape(-1))
    along_x = jnp.asarray(four_planes(pair), jnp.bfloat16)
    along_x_half = jnp.asarray(four_planes(width), jnp.bfloat16)
    along_y = jnp.asarray(np.kron(np.eye(snaps, dtype=np.float32), band(rows)), jnp.bfloat16)
    along_z = jnp.asarray(band(lanes).T, jnp.bfloat16)
    field = pltpu.VMEM((2 * size, pair), jnp.float32)

    def sums(cells, groups, extra=0):
        shape = (ORDERS, 3, cells, rows, width)
        last = -(-(ORDERS * 3 * groups + extra) // rows)
        return {
            "out_shape": [
                jax.ShapeDtypeStruct((ORDERS * 3 * cells + last, rows, width), jnp.int16),
                jax.ShapeDtypeStruct(shape, jnp.float32),
            ],
        }, [pltpu.VMEM(shape, jnp.float32), pltpu.VMEM((last * rows, width), jnp.float32)]

    def inside_sums(weights):
        call, scratch = sums(2 * planes, 4, 2 * snaps)
        return pl.pallas_call(
            inside_kernel,
            scratch_shapes=[*scratch, field, field, field, field],
            **call, **params(26),
        )(spread_bins, weights, along_x, along_y, along_z, velocity, other)

    def edge_sums(weights, components, near, halos, halo_of):
        count = len(components)

        def body(*refs):
            edge_kernel(components, near, len(halos), halo_of, *refs)

        call, scratch = sums(2 * count, count)
        return pl.pallas_call(body, scratch_shapes=[*scratch, field, field], **call, **params(26))(
            weights, along_x, along_y, along_z, velocity, other, *halos
        )

    def exchange(parts):
        code, here = parts
        return here, lax.ppermute(code, "snap", chip_pairs)

    other = lax.ppermute(velocity, "snap", core_pairs)
    with jax.named_scope("pack"):
        (near_own,) = pack(pack_near_kernel, (velocity,), [near_shape], 2, 51)
        halo_own = lax.ppermute(near_own, "slab", near_pairs)
    pair_bins = jnp.concatenate([phase_bins, lax.ppermute(phase_bins, "snap", core_pairs)])

    with jax.named_scope("weights"):
        pair_weights, spread_bins = pl.pallas_call(
            weights_kernel,
            in_specs=[smem(), smem()],
            out_shape=[
                jax.ShapeDtypeStruct((2 * snaps, 2, 8, 128), jnp.float32),
                jax.ShapeDtypeStruct((2 * snaps, width), jnp.float32),
            ],
            **params(8),
        )(pair_bins, table)
    with jax.named_scope("pack"):
        for_across, for_diagonal = pack(
            pack_across_kernel, (after(velocity, near_own),), [(snaps, 6, rows, width)] * 2, 4
        )
        across = lax.ppermute(for_across, "snap", chip_pairs)
        diagonal = lax.ppermute(for_diagonal, "snap", diagonal_pairs)
        near_other, far_w = pack(
            pack_other_kernel, (velocity, after(other, for_across, for_diagonal, pair_weights)), [near_shape, far_shape], 6
        )
        halo_other = lax.ppermute(near_other, "slab", near_pairs)

    with jax.named_scope("inside"):
        inside_parts = inside_sums(after(pair_weights, near_other, far_w))

    with jax.named_scope("pack"):
        (far_v,) = pack(
            pack_far_kernel, (velocity, after(other, inside_parts[0], halo_own), across, diagonal), [(4, snaps, 2, rows, width)], 4
        )
    inside = exchange((after(inside_parts[0], far_v), inside_parts[1]))
    halo_w = lax.ppermute(after(far_w, inside_parts[0]), "slab", far_pairs)
    halo_v = lax.ppermute(after(far_v, halo_other), "slab", far_pairs)

    with jax.named_scope("edge_near"):
        near = exchange(edge_sums(pair_weights, (1, 2), True, (halo_own, halo_other), lambda halos, g: halos[g]))
    with jax.named_scope("edge_far"):
        ready = pair_weights
        far_y = exchange(edge_sums(ready, (2,), False, (halo_w,), lambda halos, g: halos[0].at[g]))

    with jax.named_scope("invert"):
        weights, inverse = pl.pallas_call(
            invert_kernel,
            in_specs=[smem(), vmem(), vmem()],
            out_shape=[
                jax.ShapeDtypeStruct((4 * snaps, 2, 8, 128), jnp.float32),
                jax.ShapeDtypeStruct((9, rows, width), jnp.float32),
            ],
            scratch_shapes=[
                pltpu.VMEM((2 * snaps, width), jnp.int32),
                pltpu.SMEM((2 * snaps, width), jnp.int32),
                pltpu.SemaphoreType.DMA,
            ],
            **params(8),
        )(table, pair_weights, inside[1])

    out_shape = jax.ShapeDtypeStruct((3, 3, ORDERS, planes, rows, width), jnp.float32)

    lasts = 3, 2

    def one_order(parts, last):
        cells = parts[0].shape[2]
        return [
            pl.BlockSpec((1, 3, cells, rows, width), lambda p: (p, 0, 0, 0, 0)),
            pl.BlockSpec((3 * cells, rows, width), lambda p: (p, 0, 0)),
            pl.BlockSpec((last, rows, width), lambda p: (ORDERS * 3 * cells // last, 0, 0)),
        ]

    with jax.named_scope("finish"):
        out = pl.pallas_call(
            finish_kernel,
            out_shape=out_shape,
            grid=(ORDERS,),
            in_specs=[
                pl.BlockSpec((9, rows, width), lambda p: (0, 0, 0)),
                *one_order(inside, lasts[0]), *one_order(near, lasts[1]),
            ],
            out_specs=pl.BlockSpec((3, 3, 1, planes, rows, width), lambda p: (0, 0, p, 0, 0, 0)),
            scratch_shapes=[pltpu.VMEM((last * rows, width), jnp.float32) for last in lasts],
            **params(16),
        )(inverse, *inside, inside[1], *near, near[1])

    with jax.named_scope("finish_far"):
        edges = pltpu.VMEM((3, 2, ORDERS, 2, rows, width), jnp.float32)
        return pl.pallas_call(
            finish_far_kernel,
            out_shape=out_shape,
            in_specs=[vmem()] * 11 + [hbm()],
            out_specs=hbm(),
            scratch_shapes=[
                edges,
                pltpu.VMEM((rows, width), jnp.float32),
                pltpu.VMEM((4 * size, width), jnp.float32),
                pltpu.VMEM((4 * size, width), jnp.float32),
                pltpu.SemaphoreType.DMA,
            ],
            input_output_aliases={11: 0},
            **params(26),
        )(
            weights, inverse, along_x_half, along_y, velocity, other, across, diagonal,
            after(halo_v, out), *far_y, out,
        )


def solution(mesh):
    in_specs = (P("snap", None, "slab", None, None), P("snap"))
    out_specs = P(None, None, None, "slab", None, "snap")
    return jax.shard_map(local, mesh=mesh, in_specs=in_specs, out_specs=out_specs, check_vma=False)
```

```python
import jax
import jax.numpy as jnp
import numpy as np
from jax import lax
from jax.experimental import pallas as pl
from jax.experimental.pallas import tpu as pltpu
from jax.sharding import PartitionSpec as P

BINS = 180
ORDERS = 4
TAPS = ((-2, 1.0), (-1, -8.0), (1, 8.0), (2, -1.0))
STEP = 0.75 / 12.0
LEVELS = 32766.0
TINY = 1e-30


def band(size):
    matrix = np.zeros((size, size), np.float32)
    for offset, factor in TAPS:
        matrix += factor * np.eye(size, k=offset, dtype=np.float32)
    return matrix


def four_planes(width):
    return np.concatenate([factor * np.eye(width, dtype=np.float32) for _, factor in TAPS])


def halo_planes(width):
    factors = dict(TAPS)
    eye = np.eye(width, dtype=np.float32)
    return np.stack(
        [
            np.stack([np.concatenate([factors.get(4 * high + i - p - 2, 0.0) * eye for i in range(2)]) for p in range(2)])
            for high in range(2)
        ]
    )


def phase_table():
    centers = (np.arange(BINS, dtype=np.float32) + np.float32(0.5)) * np.float32(2.0 * np.pi / BINS)
    return np.stack([np.cos(centers), np.sin(centers)], axis=1).astype(np.float32)


def weights_kernel(bins, table, weight, spread):
    for s in range(bins.shape[0]):
        weight[s, 0] = jnp.full(weight.shape[2:], table[bins[s] * 2], jnp.float32)
        weight[s, 1] = jnp.full(weight.shape[2:], table[bins[s] * 2 + 1], jnp.float32)
        spread[pl.ds(s, 1), :] = jnp.full((1, spread.shape[1]), bins[s], jnp.int32).astype(jnp.float32)


def invert_kernel(table, pair_weight, code, weight, inverse, received, bins, sem):
    count = pair_weight.shape[0]
    received[...] = code[code.shape[0] - count // code.shape[1] :].astype(jnp.int32).reshape(received.shape)
    copy = pltpu.make_async_copy(received, bins, sem)
    copy.start()
    weight[:count] = pair_weight[...]
    copy.wait()
    g01 = g02 = g11 = g12 = g22 = jnp.zeros(weight.shape[2:], jnp.float32)
    for s in range(weight.shape[0]):
        if s >= count:
            row = bins[s - count, 0] * 2
            weight[s, 0] = jnp.full(weight.shape[2:], table[row], jnp.float32)
            weight[s, 1] = jnp.full(weight.shape[2:], table[row + 1], jnp.float32)
        cosine, sine = weight[s, 0], weight[s, 1]
        g01, g02 = g01 + cosine, g02 + sine
        g11, g12, g22 = g11 + cosine * cosine, g12 + cosine * sine, g22 + sine * sine
    g00 = jnp.full(weight.shape[2:], weight.shape[0], jnp.float32)
    c00 = g11 * g22 - g12 * g12
    c01 = g02 * g12 - g01 * g22
    c02 = g01 * g12 - g02 * g11
    c11 = g00 * g22 - g02 * g02
    c12 = g02 * g01 - g00 * g12
    c22 = g00 * g11 - g01 * g01
    determinant = g00 * c00 + g01 * c01 + g02 * c02
    for i, entry in enumerate((c00, c01, c02, c01, c11, c12, c02, c12, c22)):
        for half in range(inverse.shape[1] // 8):
            inverse[i, pl.ds(half * 8, 8)] = entry / determinant


class Spot:
    def __init__(self, planes):
        snap, odd = lax.axis_index("snap"), lax.rem(lax.axis_index("slab"), 2)
        chip, core = lax.div(snap, 2), lax.rem(snap, 2)
        there, here = (1 - chip) * 2, chip * 2
        self.there, self.here, self.diagonal = there + core, here + core, there + 1 - core
        self.near, self.far = Side(planes, 1 - odd), Side(planes, odd)

    def lanes(self, block):
        return lanes_from(block * 128, 128)

    def pair(self):
        return self.lanes(self.there), self.lanes(self.here)


class Side:
    def __init__(self, planes, high):
        self.high = high == 1
        self.edge, self.own, self.own_at = high * (planes - 2), high * (planes - 4), 2 - high * 2
        self.halo_at, self.edge_at = high * 4, high * 2

    def around(self, p, own, halo):
        planes = []
        for offset, _ in TAPS:
            at = p + 2 + offset
            if at < 2:
                planes.append(jnp.where(self.high, own(at), halo(at)))
            elif at < 4:
                planes.append(own(at - self.own_at))
            else:
                planes.append(jnp.where(self.high, halo(at - 4), own(at - 2)))
        return jnp.concatenate(planes, axis=1)


def lanes_from(start, size):
    return pl.ds(pl.multiple_of(start, 128), size)


def power_sums(field, weight, lane, half, rows, store):
    total = [None] * (3 * ORDERS)
    for s in range(weight.shape[0]):
        first = field[pl.ds(s * rows + half * 8, 8), pl.ds(lane, 128)]
        second = first * first
        powers = (first, second, second * first, second * second)
        for j in range(3):
            for k in range(ORDERS):
                term = powers[k] if j == 0 else powers[k] * weight[s, j - 1]
                at = j * ORDERS + k
                total[at] = term if s == 0 else total[at] + term
    store(pl.ds(half * 8, 8), [[total[j * ORDERS + k] * STEP ** (k + 1) for k in range(ORDERS)] for j in range(3)])


def pair_sums(field, weight, rows, there, here, cell):
    def piece(half, lane, target):
        def store(at, sums):
            for j in range(3):
                for k in range(ORDERS):
                    target[k, j, cell, at, :] = sums[j][k]

        power_sums(field, weight, lane, half, rows, store)

    return [
        lambda half=half, lane=lane, target=target: piece(half, lane, target)
        for lane, target in ((0, there), (128, here))
        for half in range(rows // 8)
    ]


def weave(pieces, chunks):
    done = 0
    for i, piece in enumerate(pieces):
        piece()
        while done * len(pieces) < (i + 1) * len(chunks):
            chunks[done]()
            done += 1


def encode(sums, exponents, code, groups, bins=None):
    cells, rows = sums.shape[2:4]
    exponents[...] = jnp.zeros(exponents.shape, jnp.float32)
    for n in range(ORDERS * 3):
        for g, (start, stop) in enumerate(groups):
            value = sums[n // 3, n % 3, start:stop]
            top = jnp.max(jnp.max(jnp.abs(value), axis=0), axis=0, keepdims=True)
            exponent = jnp.ceil(jnp.log(jnp.maximum(top, TINY)) * np.float32(1.0 / np.log(2.0)))
            rounded = jnp.round(value * (jnp.exp2(-exponent) * LEVELS))
            code[n * cells + start : n * cells + stop] = rounded.astype(jnp.int32).astype(jnp.int16)
            exponents[pl.ds(n * len(groups) + g, 1), :] = exponent
    if bins is not None:
        exponents[exponents.shape[0] - bins.shape[0] :] = bins[...]
    last = exponents[...].reshape(exponents.shape[0] // rows, rows, exponents.shape[1])
    code[ORDERS * 3 * cells :] = last.astype(jnp.int32).astype(jnp.int16)


def decode_scales(code, scales):
    exponents = code.astype(jnp.int32).astype(jnp.float32)
    scales[...] = (jnp.exp2(exponents) * (1.0 / LEVELS)).reshape(scales.shape)


def flat(block):
    return block.reshape(block.shape[0] * block.shape[1], block.shape[2])


def product(a, b):
    return jnp.dot(a, b, preferred_element_type=jnp.float32)


def make_copies(pairs, sems):
    return [pltpu.make_async_copy(source, target, sems.at[i]) for i, (source, target) in enumerate(pairs)]


def run_copies(pairs, sems):
    copies = make_copies(pairs, sems)
    for copy in copies:
        copy.start()
    for copy in copies:
        copy.wait()


def fill_x(field, along_y, along_z, v, w):
    size = along_y.shape[0]

    def chunk(g):
        field[pl.ds(g * size, size), :] = product(along_y[...], w(g)) - product(v(g), along_z())

    return [lambda g=g: chunk(g) for g in range(field.shape[0] // size)]


def fill_y(field, along_x, along_y, along_z, u, planes):
    size = along_y.shape[0]

    def chunk(g):
        field[pl.ds(g * size, size), :] = product(u(g), along_z()) - product(planes(g), along_x[...])

    return [lambda g=g: chunk(g) for g in range(field.shape[0] // size)]


def fill_z(field, along_x, along_y, u, planes):
    size = along_y.shape[0]

    def chunk(g):
        field[pl.ds(g * size, size), :] = product(planes(g), along_x[...]) - product(along_y[...], u(g))

    return [lambda g=g: chunk(g) for g in range(field.shape[0] // size)]


def run(chunks):
    for chunk in chunks:
        chunk()


def halves(spot, load):
    return jnp.concatenate([flat(load(block)) for block in spot.pair()], axis=1)


def inside_kernel(bins, weight, along_x, along_y, all_z, own, other, code, here, there, exponents, *fields):
    planes, rows = own.shape[2:4]
    steps = planes // 2
    spot = Spot(planes)
    sources = (own, other)

    def half(c, g, p):
        return halves(spot, lambda block: sources[g][:, c, p, :, block])

    def along_z():
        return jnp.concatenate([all_z[:, block] for block in spot.pair()], axis=1)

    def streamwise(field, p):
        return fill_x(field, along_y, along_z, lambda g: flat(sources[g][:, 1, p]), lambda g: half(2, g, p))

    def around(c, g, p):
        return jnp.concatenate([half(c, g, p + offset) for offset, _ in TAPS], axis=1)

    def summed(i, cell):
        return pair_sums(fields[i], weight, rows, there, here, cell)

    run(streamwise(fields[0], 0))

    @pl.loop(0, steps)
    def _(step):
        p = step + 2
        weave(summed(0, 2 * step), streamwise(fields[1], 2 * step + 1))
        weave(
            summed(1, 2 * step + 1),
            fill_z(fields[3], along_x, along_y, lambda g: half(0, g, p), lambda g: around(1, g, p)),
        )
        weave(
            summed(3, planes + steps + step),
            fill_y(
                fields[2], along_x, along_y, along_z,
                lambda g: flat(sources[g][:, 0, p]), lambda g: around(2, g, p),
            ),
        )
        weave(summed(2, planes + step), streamwise(fields[0], jnp.minimum(2 * step + 2, planes - 1)))

    encode(there, exponents, code, [(g * steps, g * steps + steps) for g in range(4)], bins)


def edge_kernel(components, near, n_halos, halo_of, weight, along_x, along_y, all_z, own, other, *refs):
    count = len(components)
    halos, (code, here, there, exponents, *fields) = refs[:n_halos], refs[n_halos:]
    rows = own.shape[3]
    spot = Spot(own.shape[2])
    side = spot.near if near else spot.far
    sources = (own, other)

    def along_z():
        return jnp.concatenate([all_z[:, block] for block in spot.pair()], axis=1)

    def fill(n):
        c, p = components[n // 2], n % 2

        def around(g):
            return side.around(
                p,
                lambda i: halves(spot, lambda block: sources[g][:, c, side.own + i, :, block]),
                lambda i: flat(halo_of(halos, g)[:, c - components[0], i]),
            )

        if c == 2:
            return fill_y(
                fields[n % 2], along_x, along_y, along_z, lambda g: flat(sources[g][:, 0, side.edge + p]), around
            )
        return fill_z(
            fields[n % 2], along_x, along_y,
            lambda g: halves(spot, lambda block: sources[g][:, 0, side.edge + p, :, block]), around,
        )

    run(fill(0))
    for n in range(2 * count):
        weave(
            pair_sums(fields[n % 2], weight, rows, there, here, n),
            fill(n + 1) if n + 1 < 2 * count else [],
        )
    encode(there, exponents, code, [(2 * i, 2 * i + 2) for i in range(count)])


def solve(inverse, here, code, scales, cells, group, store):
    start, stop = cells
    count, groups = here.shape[0], scales.shape[0] // 3
    depth = here.shape[1]
    sums = []
    for j in range(count):
        coded = code[j * depth + start : j * depth + stop].astype(jnp.int32).astype(jnp.float32)
        sums.append(here[j, start:stop] + coded * scales[j * groups + group : j * groups + group + 1, :])
    for i in range(3):
        store(i, inverse[3 * i] * sums[0] + inverse[3 * i + 1] * sums[1] + inverse[3 * i + 2] * sums[2])


def finish_kernel(inverse, here, code, exponents, near_here, near_code, near_exponents, out, scales, near_scales):
    planes = out.shape[3]
    half = planes // 2
    edge = pl.ds(Spot(planes).near.edge, 2)

    @pl.when(pl.program_id(0) == 0)
    def _():
        decode_scales(exponents[...], scales)
        decode_scales(near_exponents[...], near_scales)

    inner = slice(2, planes - 2)
    targets = [(0, slice(0, half)), (0, slice(half, planes)), (1, inner), (2, inner), (2, edge), (1, edge)]
    for n, (component, at) in enumerate(targets):
        def store(i, value, component=component, at=at):
            out[i, component, 0, at] = value

        if n < 4:
            own = scales.at[pl.ds(pl.program_id(0) * 12, 12)]
            solve(inverse, here.at[0], code, own, (n * half, n * half + half), n, store)
        else:
            own = near_scales.at[pl.ds(pl.program_id(0) * 6, 6)]
            solve(inverse, near_here.at[0], near_code, own, (2 * n - 8, 2 * n - 6), n - 4, store)


def far_field_kernel(along_x, along_y, own, other, across, diagonal, base):
    spot = Spot(own.shape[2])
    side, lane_here = spot.far, spot.lanes(spot.here)
    sources = (own, other, across, diagonal)

    for p in range(2):
        def u(g, p=p):
            return flat(sources[g][:, 0, side.edge + p, :, lane_here] if g < 2 else sources[g][:, 4 + p])

        def own_plane(g, i):
            return flat(sources[g][:, 1, side.own + i, :, lane_here] if g < 2 else sources[g][:, i])

        def around(g, p=p):
            nothing = jnp.zeros((along_y.shape[0], along_x.shape[1]), own.dtype)
            return side.around(p, lambda i: own_plane(g, i), lambda i: nothing)

        run(fill_z(base.at[p], along_x, along_y, u, around))


def finish_far_kernel(weight, inverse, along_halo, base, halo, *refs):
    far_here, far_code, _, out, far_out, far_scales, *fields, out_sem = refs
    parts, snaps, _, rows, _ = halo.shape
    size = snaps * rows
    side = Spot(out.shape[3]).far
    high = side.halo_at // 4

    def fill(p):
        def chunk(g):
            planes = jnp.concatenate([flat(halo[g, :, i]) for i in range(2)], axis=1)
            at = pl.ds(g * size, size)
            fields[p][at, :] = base[p, at, :] + product(planes, along_halo[high, p])

        return [lambda g=g: chunk(g) for g in range(parts)]

    def solve_order(k):
        def store_far(i, value):
            far_out[i, 0, k] = value

        scales = far_scales.at[pl.ds(3 * k, 3)]
        solve(inverse, far_here.at[k], far_code.at[pl.ds(6 * k, 6)], scales, (0, 2), 0, store_far)

    def sum_half(p, half):
        def store(at, sums):
            for k in range(ORDERS):
                for i in range(3):
                    far_out[i, 1, k, p, at, :] = (
                        inverse[3 * i, at] * sums[0][k]
                        + inverse[3 * i + 1, at] * sums[1][k]
                        + inverse[3 * i + 2, at] * sums[2][k]
                    )

        power_sums(fields[p], weight, 0, half, rows, store)

    decode_scales(far_code[ORDERS * 6 :], far_scales)
    weave([lambda k=k: solve_order(k) for k in range(ORDERS)], fill(0))
    weave([lambda half=half: sum_half(0, half) for half in range(rows // 8)], fill(1))
    for half in range(rows // 8):
        sum_half(1, half)
    copy = pltpu.make_async_copy(far_out, out.at[:, pl.ds(1, 2), :, pl.ds(side.edge, 2)], out_sem)
    copy.start()
    copy.wait()


def pack_near_kernel(own, near, sems):
    spot = Spot(own.shape[2])
    planes = pl.ds(spot.near.edge, 2)
    run_copies(
        [
            (own.at[:, pl.ds(1, 2), planes, :, block], near.at[:, :, :, :, pl.ds(b * 128, 128)])
            for b, block in enumerate(spot.pair())
        ],
        sems,
    )


def pack_across_kernel(own, across, diagonal, sems):
    spot = Spot(own.shape[2])
    pairs = []
    for target, block in ((across, spot.there), (diagonal, spot.diagonal)):
        lane = spot.lanes(block)
        pairs.append((own.at[:, 1, pl.ds(spot.far.own, 4), :, lane], target.at[:, pl.ds(0, 4)]))
        pairs.append((own.at[:, 0, pl.ds(spot.far.edge, 2), :, lane], target.at[:, pl.ds(4, 2)]))
    run_copies(pairs, sems)


def pack_other_kernel(own, other, near, far, sems):
    spot = Spot(own.shape[2])
    pairs = []
    for b, source in enumerate(spot.pair()):
        target = pl.ds(b * 128, 128)
        planes = pl.ds(spot.near.edge, 2)
        pairs.append((other.at[:, pl.ds(1, 2), planes, :, source], near.at[:, :, :, :, target]))
        planes = pl.ds(spot.far.edge, 2)
        for g, array in enumerate((own, other)):
            pairs.append((array.at[:, pl.ds(2, 1), planes, :, source], far.at[g, :, :, :, :, target]))
    run_copies(pairs, sems)


def pack_far_kernel(own, other, across, diagonal, far, sems):
    spot = Spot(own.shape[2])
    planes, lane = pl.ds(spot.far.edge, 2), spot.lanes(spot.here)
    pairs = [(array.at[:, 1, planes, :, lane], far.at[g]) for g, array in enumerate((own, other))]
    planes = pl.ds(spot.far.edge_at, 2)
    pairs += [(array.at[:, planes], far.at[2 + g]) for g, array in enumerate((across, diagonal))]
    run_copies(pairs, sems)


def params(megabytes):
    return {
        "compiler_params": pltpu.CompilerParams(vmem_limit_bytes=megabytes * 2**20),
        "cost_estimate": pl.CostEstimate(flops=1, bytes_accessed=1, transcendentals=0),
    }


def smem():
    return pl.BlockSpec(memory_space=pltpu.SMEM)


def hbm():
    return pl.BlockSpec(memory_space=pl.ANY)


def vmem():
    return pl.BlockSpec(memory_space=pltpu.VMEM)


def after(value, *others):
    return lax.optimization_barrier((value, *others))[0]


def local(velocity, phase_bins):
    snaps, _, planes, rows, lanes = velocity.shape
    kind = velocity.dtype
    n_snap, n_slab = lax.axis_size("snap"), lax.axis_size("slab")
    width = lanes // n_snap
    pair, size = 2 * width, snaps * rows

    near_pairs = [(i, i ^ 1) for i in range(n_slab)]
    far_pairs = [(i, i + 1) for i in range(1, n_slab - 1, 2)]
    far_pairs = far_pairs + [(j, i) for i, j in far_pairs]
    core_pairs = [(i, i ^ 1) for i in range(n_snap)]
    chip_pairs = [(i, (i + 2) % n_snap) for i in range(n_snap)]
    diagonal_pairs = [(i, ((i + 2) % n_snap) ^ 1) for i in range(n_snap)]

    def pack(kernel, arrays, shapes, copies, megabytes=8):
        return pl.pallas_call(
            kernel,
            in_specs=[hbm()] * len(arrays),
            out_specs=[vmem()] * len(shapes),
            out_shape=[jax.ShapeDtypeStruct(shape, kind) for shape in shapes],
            scratch_shapes=[pltpu.SemaphoreType.DMA((copies,))],
            **params(megabytes),
        )(*arrays)

    near_shape, far_shape = (snaps, 2, 2, rows, pair), (2, snaps, 1, 2, rows, pair)
    table = jnp.asarray(phase_table().reshape(-1))
    along_x = jnp.asarray(four_planes(pair), jnp.bfloat16)
    along_x_half = jnp.asarray(four_planes(width), jnp.bfloat16)
    along_y = jnp.asarray(np.kron(np.eye(snaps, dtype=np.float32), band(rows)), jnp.bfloat16)
    along_z = jnp.asarray(band(lanes).T, jnp.bfloat16)
    field = pltpu.VMEM((2 * size, pair), jnp.float32)

    def sums(cells, groups, extra=0):
        shape = (ORDERS, 3, cells, rows, width)
        last = -(-(ORDERS * 3 * groups + extra) // rows)
        return {
            "out_shape": [
                jax.ShapeDtypeStruct((ORDERS * 3 * cells + last, rows, width), jnp.int16),
                jax.ShapeDtypeStruct(shape, jnp.float32),
            ],
        }, [pltpu.VMEM(shape, jnp.float32), pltpu.VMEM((last * rows, width), jnp.float32)]

    def inside_sums(weights):
        call, scratch = sums(2 * planes, 4, 2 * snaps)
        return pl.pallas_call(
            inside_kernel,
            scratch_shapes=[*scratch, field, field, field, field],
            **call, **params(26),
        )(spread_bins, weights, along_x, along_y, along_z, velocity, other)

    def edge_sums(weights, components, near, halos, halo_of):
        count = len(components)

        def body(*refs):
            edge_kernel(components, near, len(halos), halo_of, *refs)

        call, scratch = sums(2 * count, count)
        return pl.pallas_call(body, scratch_shapes=[*scratch, field, field], **call, **params(26))(
            weights, along_x, along_y, along_z, velocity, other, *halos
        )

    def exchange(parts):
        code, here = parts
        return here, lax.ppermute(code, "snap", chip_pairs)

    other = lax.ppermute(velocity, "snap", core_pairs)
    with jax.named_scope("pack"):
        (near_own,) = pack(pack_near_kernel, (velocity,), [near_shape], 2, 51)
        halo_own = lax.ppermute(near_own, "slab", near_pairs)
    pair_bins = jnp.concatenate([phase_bins, lax.ppermute(phase_bins, "snap", core_pairs)])

    with jax.named_scope("weights"):
        pair_weights, spread_bins = pl.pallas_call(
            weights_kernel,
            in_specs=[smem(), smem()],
            out_shape=[
                jax.ShapeDtypeStruct((2 * snaps, 2, 8, 128), jnp.float32),
                jax.ShapeDtypeStruct((2 * snaps, width), jnp.float32),
            ],
            **params(8),
        )(pair_bins, table)
    with jax.named_scope("pack"):
        for_across, for_diagonal = pack(
            pack_across_kernel, (after(velocity, near_own),), [(snaps, 6, rows, width)] * 2, 4
        )
        across = lax.ppermute(for_across, "snap", chip_pairs)
        diagonal = lax.ppermute(for_diagonal, "snap", diagonal_pairs)
        near_other, far_w = pack(
            pack_other_kernel, (velocity, after(other, for_across, for_diagonal, pair_weights)), [near_shape, far_shape], 6
        )
        halo_other = lax.ppermute(near_other, "slab", near_pairs)

    with jax.named_scope("inside"):
        inside_parts = inside_sums(after(pair_weights, near_other, far_w))

    with jax.named_scope("pack"):
        (far_v,) = pack(
            pack_far_kernel, (velocity, after(other, inside_parts[0], halo_own), across, diagonal), [(4, snaps, 2, rows, width)], 4
        )
    inside = exchange((after(inside_parts[0], far_v), inside_parts[1]))
    halo_w = lax.ppermute(after(far_w, inside_parts[0]), "slab", far_pairs)
    halo_v = lax.ppermute(after(far_v, halo_other), "slab", far_pairs)

    with jax.named_scope("edge_near"):
        near = exchange(edge_sums(pair_weights, (1, 2), True, (halo_own, halo_other), lambda halos, g: halos[g]))
    with jax.named_scope("edge_far"):
        ready = pair_weights
        far_y = exchange(edge_sums(ready, (2,), False, (halo_w,), lambda halos, g: halos[0].at[g]))

    with jax.named_scope("invert"):
        weights, inverse = pl.pallas_call(
            invert_kernel,
            in_specs=[smem(), vmem(), vmem()],
            out_shape=[
                jax.ShapeDtypeStruct((4 * snaps, 2, 8, 128), jnp.float32),
                jax.ShapeDtypeStruct((9, rows, width), jnp.float32),
            ],
            scratch_shapes=[
                pltpu.VMEM((2 * snaps, width), jnp.int32),
                pltpu.SMEM((2 * snaps, width), jnp.int32),
                pltpu.SemaphoreType.DMA,
            ],
            **params(8),
        )(table, pair_weights, inside[1])

    out_shape = jax.ShapeDtypeStruct((3, 3, ORDERS, planes, rows, width), jnp.float32)

    lasts = 3, 2

    def one_order(parts, last):
        cells = parts[0].shape[2]
        return [
            pl.BlockSpec((1, 3, cells, rows, width), lambda p: (p, 0, 0, 0, 0)),
            pl.BlockSpec((3 * cells, rows, width), lambda p: (p, 0, 0)),
            pl.BlockSpec((last, rows, width), lambda p: (ORDERS * 3 * cells // last, 0, 0)),
        ]

    with jax.named_scope("finish"):
        out = pl.pallas_call(
            finish_kernel,
            out_shape=out_shape,
            grid=(ORDERS,),
            in_specs=[
                pl.BlockSpec((9, rows, width), lambda p: (0, 0, 0)),
                *one_order(inside, lasts[0]), *one_order(near, lasts[1]),
            ],
            out_specs=pl.BlockSpec((3, 3, 1, planes, rows, width), lambda p: (0, 0, p, 0, 0, 0)),
            scratch_shapes=[pltpu.VMEM((last * rows, width), jnp.float32) for last in lasts],
            **params(16),
        )(inverse, *inside, inside[1], *near, near[1])

    with jax.named_scope("far_field"):
        base = pl.pallas_call(
            far_field_kernel,
            out_shape=jax.ShapeDtypeStruct((2, 4 * size, width), jnp.float32),
            **params(26),
        )(after(along_x_half, near[0]), along_y, velocity, other, across, diagonal)

    with jax.named_scope("finish_far"):
        edges = pltpu.VMEM((3, 2, ORDERS, 2, rows, width), jnp.float32)
        return pl.pallas_call(
            finish_far_kernel,
            out_shape=out_shape,
            in_specs=[vmem()] * 7 + [hbm()],
            out_specs=hbm(),
            scratch_shapes=[
                edges,
                pltpu.VMEM((rows, width), jnp.float32),
                pltpu.VMEM((4 * size, width), jnp.float32),
                pltpu.VMEM((4 * size, width), jnp.float32),
                pltpu.SemaphoreType.DMA,
            ],
            input_output_aliases={7: 0},
            **params(26),
        )(
            weights, inverse, jnp.asarray(halo_planes(width), jnp.bfloat16), base, after(halo_v, out), *far_y, out
        )


def solution(mesh):
    in_specs = (P("snap", None, "slab", None, None), P("snap"))
    out_specs = P(None, None, None, "slab", None, "snap")
    return jax.shard_map(local, mesh=mesh, in_specs=in_specs, out_specs=out_specs, check_vma=False)
```
